256 devices in a mesh: dp: 32 (over y, z), cent: 8 (over x, core).
Axes of the slice: x: 4, y: 4, z: 8, core: 2. Of those that a mesh axis runs over, the one named last changes fastest.
Arguments:
- stream: bfloat16 [65536, 768], P('dp'), may hold values from -6 to 6
- sample_index: int32 [32768], P('dp'), may hold values from 0 to 2047
- centroids: float32 [16384, 768], P(('cent', 'dp')), may hold values from -6 to 6
- first_moment: float32 [16384, 768], P(('cent', 'dp')), may hold values from -3 to 3
- second_moment: float32 [16384, 768], P(('cent', 'dp')), may hold values from 0.01 to 1
Outputs:
- new_centroids: float32 [16384, 768], P(('cent', 'dp'))
- new_first: float32 [16384, 768], P(('cent', 'dp'))
- new_second: float32 [16384, 768], P(('cent', 'dp'))
The draws below stay inside these ranges and needn't reach their ends.
All inputs are finite; a program needn't handle non-finite values.
Results may differ from the reference program's by a relative error of at most 0.0003.
Values may be sent and summed in bfloat16 or wider, within the bound.
A program may use at most 64 MiB of HBM per device.

```python
import math
import jax
import jax.numpy as jnp
from jax import lax

E = 768
KB = 16384
ND = 1024
ITERS = 3
ROWS = 32768
STREAM = 65536
N_DP = 32


def distant_rows(key):
    placed = jax.random.permutation(jax.random.fold_in(key, 11), KB)[:8].astype(jnp.int32)
    flips = jax.random.bernoulli(jax.random.fold_in(key, 12), 0.5, (8, E))
    signs = jnp.where(flips, 1.0, -1.0).astype(jnp.float32)
    levels = jnp.array([0.75, 1.0, 1.25, 1.5, 0.75, 1.0, 1.25, 1.5], jnp.float32) * jnp.sqrt(768.0 / E)
    return (placed, levels[:, None] * signs)


def draw_stream(key, part):
    drawn_values = jnp.clip(jax.random.normal(jax.random.fold_in(key, 1), (STREAM, E), jnp.float32), -6.0, 6.0)
    return drawn_values.astype(jnp.bfloat16)


def draw_centroids(key, part):
    drawn_values = jnp.clip(0.1 * jax.random.normal(jax.random.fold_in(key, 2), (KB, E), jnp.float32), -0.6, 0.6)
    placed, distant = distant_rows(key)
    drawn_values = drawn_values.at[placed].set(distant)
    return drawn_values


def touch_ends(drawn, stream_key, low, largest):
    longest = drawn.shape.index(max(drawn.shape))
    spots = []
    for shift in (0, 1):
        where = [jax.random.randint(jax.random.fold_in(stream_key, axis), (), 0, length) for axis, length in enumerate(drawn.shape)]
        where[longest] = (where[longest] + shift) % drawn.shape[longest]
        spots.append(tuple(where))
    return drawn.at[spots[0]].set(low).at[spots[1]].set(largest)


def steps_of(own_key, shape, split, low, top_value):
    def one(dim, shards_of):
        heights = jax.random.uniform(jax.random.fold_in(jax.random.fold_in(own_key, 6), dim), (shards_of,), jnp.float32, low / len(split), top_value / len(split))
        return jnp.repeat(jnp.exp(heights), shape[dim] // shards_of).reshape((-1,) + (1,) * (len(shape) - dim - 1))

    level = one(*split[0])
    for cut in split[1:]:
        level = level * one(*cut)
    return level


def noise(own_key, dims, scale, limit, pieces=(), kind=jnp.bfloat16):
    values = scale * jax.random.normal(own_key, dims, jnp.float32)
    if pieces:
        values = values * steps_of(own_key, dims, pieces, -0.22, 0.18)
    return jnp.clip(values, -limit, limit).astype(kind)


def setup_inputs(seed: int = 0) -> dict:
    streams_of = jax.random.split(jax.random.key(seed), 6)
    stream = draw_stream(jax.random.fold_in(streams_of[5], 71), 0)
    sample_index = touch_ends(jax.random.randint(streams_of[1], (ROWS,), 0, 2 * ND), jax.random.fold_in(streams_of[1], 1), 0, (2 * ND) - 1).astype(jnp.int32)
    centroids = draw_centroids(jax.random.fold_in(streams_of[5], 71), 0)
    first_moment = noise(streams_of[3], (KB, E), 0.5, 3.0, ((0, 256),), jnp.float32)
    second_moment = jnp.clip(jnp.exp(math.log(1.0) - 4.6051702 * jax.random.uniform(streams_of[4], (KB, E), jnp.float32) ** steps_of(streams_of[4], (KB, E), ((0, 256),), -0.2, 0.2)), 0.01, 1.0)
    return {"stream": stream, "sample_index": sample_index, "centroids": centroids, "first_moment": first_moment, "second_moment": second_moment}


temper = 2.0
beta_one = 0.9
beta_two = 0.99
step_rate = 0.05
epsilon = 1e-08

def logits_of(row_block, rounded, squares):
    product = jnp.dot(row_block, rounded.T, preferred_element_type=jnp.float32)
    return (2.0 * product - squares[None, :]) / temper

def row_potential(logits, column_pot):
    shifted = logits + column_pot[None, :]
    highest = lax.optimization_barrier(jnp.max(shifted, axis=1))
    return -(highest + jnp.log(lax.optimization_barrier(jnp.sum(jnp.exp(shifted - highest[:, None]), axis=1))))

def reference(stream, sample_index, centroids, first_moment, second_moment):
    row_ids = jnp.arange(ROWS, dtype=jnp.int32)
    global_rows = (row_ids // ND * (2 * ND) + sample_index).astype(jnp.int32)
    embedded = stream[global_rows].reshape(N_DP, ND, E)
    rounded = centroids.astype(jnp.bfloat16)
    squares = lax.optimization_barrier(jnp.sum(rounded.astype(jnp.float32) ** 2, axis=1))
    balance = math.log(ROWS / KB)

    def column_pass(column_pot):

        def visit(running, row_block):
            logits = logits_of(row_block, rounded, squares)
            row_pot = row_potential(logits, column_pot)
            shifted = logits + row_pot[:, None]
            highest = lax.optimization_barrier(jnp.max(shifted, axis=0))
            summed = lax.optimization_barrier(jnp.sum(jnp.exp(shifted - highest[None, :]), axis=0))
            merged_peak = jnp.maximum(running[0], highest)
            merged_total = running[1] * jnp.exp(running[0] - merged_peak) + summed * jnp.exp(highest - merged_peak)
            return ((merged_peak, merged_total), None)
        initial = (jnp.full((KB,), -1e+30, jnp.float32), jnp.zeros((KB,), jnp.float32))
        (highest, summed), _ = lax.scan(visit, initial, embedded)
        return balance - (highest + jnp.log(summed))
    column_pot = jnp.zeros((KB,), jnp.float32)
    for sweep_index in range(ITERS):
        column_pot = column_pass(column_pot)

    def gather_stats(running, row_block):
        logits = logits_of(row_block, rounded, squares)
        row_pot = row_potential(logits, column_pot)
        transport = jnp.exp(logits + row_pot[:, None] + column_pot[None, :]).astype(jnp.bfloat16)
        weighted = running[0] + jnp.dot(transport.T, row_block, preferred_element_type=jnp.float32)
        weight_mass = running[1] + lax.optimization_barrier(jnp.sum(transport.astype(jnp.float32), axis=0))
        return ((weighted, weight_mass), None)
    initial = (jnp.zeros((KB, E), jnp.float32), jnp.zeros((KB,), jnp.float32))
    (weighted, weight_mass), _ = lax.scan(gather_stats, initial, embedded)
    gradient = (weight_mass[:, None] * centroids - weighted) * (KB / ROWS)
    new_first = beta_one * first_moment + (1.0 - beta_one) * gradient
    new_second = beta_two * second_moment + (1.0 - beta_two) * gradient * gradient
    new_centroids = centroids - step_rate * new_first / (jnp.sqrt(new_second) + epsilon)
    return (new_centroids, new_first, new_second)
```

```python
import functools
import math

import jax
import jax.numpy as jnp
from jax import lax
from jax.experimental import pallas as pl
from jax.experimental.pallas import tpu as pltpu
from jax.sharding import PartitionSpec as P

MESH = pl.DeviceIdType.MESH

KB = 16384
ROWS = 32768
NX, NY, NZ = 4, 4, 8
E = 768
OWN = 64
COLS = OWN * NZ
ND = 1024
BLK = 128
SLOTS = NY * ND // BLK
NR = SLOTS * BLK
STREAM = 2 * ND
BALANCE = math.log(ROWS / KB)
SUM_TYPE = jnp.float32
HALF = E // 2

beta_one = 0.9
beta_two = 0.99
step_rate = 0.05
epsilon = 1e-08


def pick(i, values):
    chosen = values[0]
    for k, value in enumerate(values[1:], 1):
        chosen = jnp.where(i == k, value, chosen)
    return chosen


def kernel(
    stream, idx, cent, grad,
    emb, piece, logits, transport, half_sq, col_part, col_part2, col_vec,
    row_vec, row_buf0, row_buf, row_sums, y_vec, y_buf0, y_buf, pot,
    col_send0, col_send, col_buf0, col_buf,
    partial, long_out, short_out, long_in, short_in,
    emb_send, emb_recv, sib_send, sib_recv, z_send, z_recv,
    row_send_sem, row_recv_sem, y_send_sem, y_recv_sem, col_send_sem, col_recv_sem,
    long_send_sem, long_recv_sem, short_send_sem, short_recv_sem,
):
    dp = lax.axis_index("dp")
    group = lax.axis_index("cent")
    y, z = dp // NZ, lax.rem(dp, NZ)
    x, core = group // 2, lax.rem(group, 2)

    def at_y(k):
        return {"dp": lax.rem(y + k + NY, NY) * NZ + z, "cent": group}

    def at_z(k):
        return {"dp": y * NZ + lax.rem(z + k + NZ, NZ), "cent": group}

    def at_x(k):
        return {"dp": dp, "cent": lax.rem(x + k + NX, NX) * 2 + core}

    def at_group(k):
        return {"dp": dp, "cent": lax.rem(group + k, 2 * NX)}

    sibling = {"dp": dp, "cent": x * 2 + 1 - core}

    barrier = pltpu.get_barrier_semaphore()
    for k in range(1, 2 * NX):
        pl.semaphore_signal(barrier, inc=1, device_id=at_group(k), device_id_type=MESH)
    for k in range(1, NY):
        pl.semaphore_signal(barrier, inc=1, device_id=at_y(k), device_id_type=MESH)
    for k in range(1, NZ):
        pl.semaphore_signal(barrier, inc=1, device_id=at_z(k), device_id_type=MESH)

    pending = []

    def send(src, dst, send_sem, recv_sem, device):
        copy = pltpu.make_async_remote_copy(
            src_ref=src, dst_ref=dst, send_sem=send_sem, recv_sem=recv_sem,
            device_id=device, device_id_type=MESH,
        )
        copy.start()
        pending.append(copy)

    def arrived(dst, recv_sem):
        pltpu.make_async_remote_copy(
            src_ref=dst, dst_ref=dst, send_sem=recv_sem, recv_sem=recv_sem,
            device_id=sibling, device_id_type=MESH,
        ).wait_recv()

    def slot_of(k, c, j):
        return lax.rem(y + k + NY, NY) * 8 + c * 4 + lax.rem(x + j, 4)

    def emb_at(slot, count=1):
        return emb.at[pl.ds(pl.multiple_of(slot * BLK, BLK), count * BLK), :]

    sends = [0]

    def send_block(slot, device):
        send(emb_at(slot), emb_at(slot), emb_send.at[sends[0]], emb_recv.at[slot], device)
        sends[0] += 1

    def wait_block(slot):
        arrived(emb_at(slot), emb_recv.at[slot])

    def piece_at(k):
        return piece.at[pl.ds(pl.multiple_of(lax.rem(z + k + NZ, NZ) * OWN, OWN), OWN), :]

    z_sends = [0]

    def send_piece(k, toward):
        owner = lax.rem(z + k + NZ, NZ)
        send(piece_at(k), piece_at(k), z_send.at[z_sends[0]], z_recv.at[owner], at_z(toward))
        z_sends[0] += 1

    def wait_piece(k):
        arrived(piece_at(k), z_recv.at[lax.rem(z + k + NZ, NZ)])

    def gather(j):
        quarter = lax.rem(x + j, 4)
        picked = idx[pl.ds(core * 4 + quarter, 1), :].astype(jnp.float32)
        column = jnp.broadcast_to(picked, (BLK, BLK)).T[:, :1]
        place = lax.broadcasted_iota(jnp.int32, (BLK, STREAM), 1).astype(jnp.float32)
        one_hot = jnp.where(place == column, 1.0, 0.0).astype(jnp.bfloat16)
        rows = jnp.dot(one_hot, stream[...], preferred_element_type=jnp.float32)
        slot = slot_of(0, core, j)
        emb[pl.ds(pl.multiple_of(slot * BLK, BLK), BLK), :] = rows.astype(jnp.bfloat16)
        return slot

    piece[pl.ds(pl.multiple_of(z * OWN, OWN), OWN), :] = cent[...].astype(jnp.bfloat16)
    first = gather(0)
    pl.semaphore_wait(barrier, 2 * NX + NY + NZ - 3)
    send_block(first, at_y(1))
    send_block(first, at_y(-1))
    send_piece(0, 1)
    send_piece(0, -1)
    second = gather(2)
    send_block(second, at_y(1))
    send_block(second, at_y(-1))
    gather(1)
    gather(3)
    own_first = y * 8 + core * 4
    send(emb_at(own_first, 4), emb_at(own_first, 4), sib_send, sib_recv, sibling)

    def on_piece(k, forward):
        wait_piece(k)
        if forward:
            send_piece(k, 1 if k < 0 else -1)

    def on_block(k, j, forward=(), spread=False):
        slot = slot_of(k, core, j)
        wait_block(slot)
        for toward in forward:
            send_block(slot, at_y(toward))
        if spread:
            send_block(slot, at_x(1))
            send_block(slot, at_x(-1))
        send_block(slot, sibling)

    def score(slot):
        lanes = pl.ds(pl.multiple_of(slot * BLK, BLK), BLK)
        rows = emb[pl.ds(pl.multiple_of(slot * BLK, BLK), BLK), :]
        product = lax.dot_general(
            piece[...], rows, (((1,), (1,)), ((), ())), preferred_element_type=jnp.float32
        )
        values = product - half_sq[...]
        logits[:, lanes] = values
        highest = jnp.max(values, axis=0, keepdims=True)
        row_vec[0:1, lanes] = highest
        row_vec[1:2, lanes] = jnp.sum(jnp.exp(values - highest), axis=0, keepdims=True)

    def score_all(offsets, c, wait):
        slots = [slot_of(k, c, j) for k, j in offsets]

        def body(i, carry):
            slot = pick(i, slots)
            if wait:
                wait_block(slot)
            score(slot)
            return carry

        lax.fori_loop(0, len(slots), body, 0)

    wave1 = [(-1, 0), (1, 0)]
    wave2 = [(2, 0), (-1, 1), (-1, 3), (1, 2)]
    wave3 = [(1, 1), (1, 3), (-1, 2), (2, 2)]
    wave4 = [(2, 1), (2, 3)]

    on_piece(-1, True)
    on_piece(1, True)
    on_block(-1, 0, forward=(1,), spread=True)
    on_block(1, 0, spread=True)
    on_piece(-2, True)
    on_piece(2, True)
    on_piece(-3, True)
    on_piece(3, False)
    on_block(2, 0, spread=True)
    on_block(1, 2, forward=(-1,))
    on_block(-1, 1)
    on_block(-1, 3)
    on_piece(-4, False)
    whole = piece[...].astype(jnp.float32)
    half_sq[...] = jnp.broadcast_to(
        0.5 * jnp.sum(whole * whole, axis=1, keepdims=True), (COLS, BLK)
    )
    score_all([(0, 0), (0, 1), (0, 2), (0, 3)], core, False)
    score_all(wave1, core, False)
    arrived(emb_at(y * 8 + (1 - core) * 4, 4), sib_recv)
    score_all([(0, 0), (0, 1), (0, 2), (0, 3)], 1 - core, False)
    score_all(wave1, 1 - core, True)
    score_all(wave2, core, False)
    for k, j in wave3:
        on_block(k, j)
    score_all(wave2, 1 - core, True)
    score_all(wave3, core, False)
    for k, j in wave4:
        on_block(k, j)
    score_all(wave3, 1 - core, True)
    score_all(wave4, core, False)
    score_all(wave4, 1 - core, True)

    def exchange_group(src, bufs, which):
        bufs[group] = src[...]
        for k in range(1, 2 * NX):
            send(
                src, bufs.at[group],
                row_send_sem.at[which, k - 1], row_recv_sem.at[which, group], at_group(k),
            )
        for k in range(1, 2 * NX):
            other = lax.rem(group + k, 2 * NX)
            arrived(bufs.at[other], row_recv_sem.at[which, other])

    def exchange_y(src, bufs, which):
        bufs[y] = src[...]
        for k in range(1, NY):
            send(
                src, bufs.at[y],
                y_send_sem.at[which, k - 1], y_recv_sem.at[which, y], at_y(k),
            )
        for k in range(1, NY):
            other = lax.rem(y + k, NY)
            arrived(bufs.at[other], y_recv_sem.at[which, other])

    def exchange_z(src, bufs, which):
        bufs[z] = src[...]
        for k in range(1, NZ):
            send(
                src, bufs.at[z],
                col_send_sem.at[which, k - 1], col_recv_sem.at[which, z], at_z(k),
            )
        for k in range(1, NZ):
            other = lax.rem(z + k, NZ)
            arrived(bufs.at[other], col_recv_sem.at[which, other])

    def merged(bufs, n):
        highest = bufs[0, 0:1, :]
        for k in range(1, n):
            highest = jnp.maximum(highest, bufs[k, 0:1, :])
        total = jnp.zeros_like(highest)
        for k in range(n):
            total = total + bufs[k, 1:2, :] * jnp.exp(bufs[k, 0:1, :] - highest)
        return highest, total

    def added(bufs, n):
        total = bufs[0]
        for k in range(1, n):
            total = total + bufs[k]
        return total

    def to_lanes(part):
        return jnp.transpose(part)

    def to_columns(vec):
        return jnp.transpose(jnp.broadcast_to(vec, (BLK, COLS)))

    exchange_group(row_vec, row_buf0, 0)
    highest, total = merged(row_buf0, 2 * NX)
    y_vec[0:1, :] = highest
    y_vec[1:2, :] = total
    exchange_y(y_vec, y_buf0, 0)
    highest, total = merged(y_buf0, NY)
    pot[...] = -(highest + jnp.log(total))

    def column_stats(g, carry):
        rows = pl.ds(pl.multiple_of(g * 8, 8), 8)
        tiles = [
            logits[rows, k * BLK:(k + 1) * BLK] + pot[:, k * BLK:(k + 1) * BLK] for k in range(SLOTS)
        ]
        highest = tiles[0]
        for tile in tiles[1:]:
            highest = jnp.maximum(highest, tile)
        total = jnp.exp(tiles[0] - highest)
        for tile in tiles[1:]:
            total = total + jnp.exp(tile - highest)
        col_part[rows, :] = highest
        col_part2[rows, :] = total
        return carry

    lax.fori_loop(0, COLS // 8, column_stats, 0)
    peaks = to_lanes(col_part[...])
    sums = to_lanes(col_part2[...])
    highest = jnp.max(peaks, axis=0, keepdims=True)
    col_send0[0:1, :] = highest
    col_send0[1:2, :] = jnp.sum(sums * jnp.exp(peaks - highest), axis=0, keepdims=True)
    exchange_z(col_send0, col_buf0, 0)
    highest, total = merged(col_buf0, NZ)
    col_vec[...] = to_columns(BALANCE - (highest + jnp.log(total)))

    WIDE = 2 * BLK

    def first_rows(t, carry):
        lanes = pl.ds(pl.multiple_of(t * WIDE, WIDE), WIDE)
        col = col_vec[...]
        both = jnp.concatenate([col, col], axis=1)
        plan = jnp.exp(logits[:, lanes] + pot[:, lanes] + both)
        logits[:, lanes] = plan
        row_sums[:, lanes] = jnp.sum(plan, axis=0, keepdims=True)
        return carry

    def later_rows(t, carry):
        lanes = pl.ds(pl.multiple_of(t * WIDE, WIDE), WIDE)
        col = col_vec[...]
        both = jnp.concatenate([col, col], axis=1)
        row_sums[:, lanes] = jnp.sum(logits[:, lanes] * both, axis=0, keepdims=True)
        return carry

    def row_factor(which):
        row_vec1 = row_buf.at[which - 1]
        y_bufs = y_buf.at[which - 1]
        src = row_src.at[which - 1]
        src[...] = row_sums[...]
        exchange_group(src, row_vec1, which)
        mid = y_src.at[which - 1]
        mid[...] = added(row_vec1, 2 * NX)
        exchange_y(mid, y_bufs, which)
        pot[...] = 1.0 / added(y_bufs, NY)

    row_src = row_buf.at[:, 2 * NX]
    y_src = y_buf.at[:, NY]

    def column_sums(g, carry):
        rows = pl.ds(pl.multiple_of(g * 32, 32), 32)
        total = logits[rows, 0:BLK] * pot[:, 0:BLK]
        for k in range(1, SLOTS):
            total = total + logits[rows, k * BLK:(k + 1) * BLK] * pot[:, k * BLK:(k + 1) * BLK]
        col_part[rows, :] = total
        return carry

    def column_total(which):
        src = col_send.at[which - 1]
        src[...] = jnp.sum(to_lanes(col_part[...]), axis=0, keepdims=True)
        bufs = col_buf.at[which - 1]
        exchange_z(src, bufs, which)
        return added(bufs, NZ)

    lax.fori_loop(0, NR // WIDE, first_rows, 0)
    row_factor(1)
    for sweep in (1, 2):
        lax.fori_loop(0, COLS // 32, column_sums, 0)
        col_vec[...] = to_columns((ROWS / KB) / column_total(sweep))
        lax.fori_loop(0, NR // WIDE, later_rows, 0)
        row_factor(sweep + 1)

    def make_transport(g, carry):
        rows = pl.ds(pl.multiple_of(g * 32, 32), 32)
        col = col_vec[rows, :]
        mass = jnp.zeros((32, BLK), jnp.float32)
        for k in range(SLOTS):
            lanes = slice(k * BLK, (k + 1) * BLK)
            rounded = (logits[rows, lanes] * pot[:, lanes] * col).astype(jnp.bfloat16)
            transport[rows, lanes] = rounded
            mass = mass + rounded.astype(jnp.float32)
        col_part[rows, :] = mass
        return carry

    lax.fori_loop(0, COLS // 32, make_transport, 0)

    def weigh(d0, d1):
        def rows_of(d):
            return transport[pl.ds(pl.multiple_of(lax.rem(z + d + NZ, NZ) * OWN, OWN), OWN), :]

        left = jnp.concatenate([rows_of(d0), rows_of(d1)], axis=0)

        def body(n, carry):
            lanes = pl.ds(pl.multiple_of(n * 256, 256), 256)
            both = jnp.dot(left, emb[:, lanes], preferred_element_type=jnp.float32)
            partial[d0 % NZ, :, lanes] = both[:OWN]
            partial[d1 % NZ, :, lanes] = both[OWN:]
            return carry

        lax.fori_loop(0, E // 256, body, 0)

    def features(h):
        return slice(h * HALF, (h + 1) * HALF)

    def long_step(h, s):
        way = 1 - 2 * h
        value = partial[(way * (4 - s)) % NZ, :, features(h)]
        if s:
            arrived(long_in.at[h * 4 + s - 1], long_recv_sem.at[h * 4 + s - 1])
            value = value + long_in[h * 4 + s - 1].astype(jnp.float32)
        at = h * 4 + s
        long_out[at] = value.astype(SUM_TYPE)
        send(long_out.at[at], long_in.at[at], long_send_sem.at[at], long_recv_sem.at[at], at_z(way))

    def short_step(h, s):
        way = 2 * h - 1
        value = partial[(way * (3 - s)) % NZ, :, features(h)]
        if s:
            arrived(short_in.at[h * 3 + s - 1], short_recv_sem.at[h * 3 + s - 1])
            value = value + short_in[h * 3 + s - 1].astype(jnp.float32)
        at = h * 3 + s
        short_out[at] = value.astype(SUM_TYPE)
        send(short_out.at[at], short_in.at[at], short_send_sem.at[at], short_recv_sem.at[at], at_z(way))

    weigh(4, 3)
    long_step(0, 0)
    long_step(1, 0)
    short_step(1, 0)
    weigh(-3, 2)
    short_step(0, 0)
    weigh(-2, 1)
    long_step(0, 1)
    long_step(1, 1)
    short_step(0, 1)
    short_step(1, 1)
    weigh(-1, 0)
    col_vec[...] = to_columns(column_total(3))
    long_step(0, 2)
    long_step(1, 2)
    short_step(0, 2)
    short_step(1, 2)
    long_step(0, 3)
    long_step(1, 3)
    mass = col_vec[pl.ds(pl.multiple_of(z * OWN, OWN), OWN), :][:, :1]
    for h in (0, 1):
        arrived(short_in.at[h * 3 + 2], short_recv_sem.at[h * 3 + 2])
        weighted = partial[0, :, features(h)] + short_in[h * 3 + 2].astype(jnp.float32)
        arrived(long_in.at[h * 4 + 3], long_recv_sem.at[h * 4 + 3])
        weighted = weighted + long_in[h * 4 + 3].astype(jnp.float32)
        grad[:, features(h)] = (mass * cent[:, features(h)] - weighted) * (KB / ROWS)

    for copy in pending:
        copy.wait_send()


def per_device(stream, sample_index, centroids, first_moment, second_moment):
    f32 = jnp.float32
    scratch = [
        pltpu.VMEM((NR, E), jnp.bfloat16),
        pltpu.VMEM((COLS, E), jnp.bfloat16),
        pltpu.VMEM((COLS, NR), f32),
        pltpu.VMEM((COLS, NR), jnp.bfloat16),
        pltpu.VMEM((COLS, BLK), f32),
        pltpu.VMEM((COLS, BLK), f32),
        pltpu.VMEM((COLS, BLK), f32),
        pltpu.VMEM((COLS, BLK), f32),
        pltpu.VMEM((2, NR), f32),
        pltpu.VMEM((2 * NX, 2, NR), f32),
        pltpu.VMEM((3, 2 * NX + 1, 1, NR), f32),
        pltpu.VMEM((1, NR), f32),
        pltpu.VMEM((2, NR), f32),
        pltpu.VMEM((NY, 2, NR), f32),
        pltpu.VMEM((3, NY + 1, 1, NR), f32),
        pltpu.VMEM((1, NR), f32),
        pltpu.VMEM((2, COLS), f32),
        pltpu.VMEM((3, 1, COLS), f32),
        pltpu.VMEM((NZ, 2, COLS), f32),
        pltpu.VMEM((3, NZ, 1, COLS), f32),
        pltpu.VMEM((NZ, OWN, E), f32),
        pltpu.VMEM((8, OWN, HALF), SUM_TYPE),
        pltpu.VMEM((6, OWN, HALF), SUM_TYPE),
        pltpu.VMEM((8, OWN, HALF), SUM_TYPE),
        pltpu.VMEM((6, OWN, HALF), SUM_TYPE),
        pltpu.SemaphoreType.DMA((24,)),
        pltpu.SemaphoreType.DMA((SLOTS,)),
        pltpu.SemaphoreType.DMA,
        pltpu.SemaphoreType.DMA,
        pltpu.SemaphoreType.DMA((7,)),
        pltpu.SemaphoreType.DMA((NZ,)),
        pltpu.SemaphoreType.DMA((4, 2 * NX - 1)),
        pltpu.SemaphoreType.DMA((4, 2 * NX)),
        pltpu.SemaphoreType.DMA((4, NY - 1)),
        pltpu.SemaphoreType.DMA((4, NY)),
        pltpu.SemaphoreType.DMA((4, NZ - 1)),
        pltpu.SemaphoreType.DMA((4, NZ)),
        pltpu.SemaphoreType.DMA((8,)),
        pltpu.SemaphoreType.DMA((8,)),
        pltpu.SemaphoreType.DMA((6,)),
        pltpu.SemaphoreType.DMA((6,)),
    ]
    gradient = pl.pallas_call(
        kernel,
        out_shape=jax.ShapeDtypeStruct((OWN, E), f32),
        in_specs=[pl.BlockSpec(memory_space=pltpu.VMEM)] * 3,
        out_specs=pl.BlockSpec(memory_space=pltpu.VMEM),
        scratch_shapes=scratch,
        compiler_params=pltpu.CompilerParams(
            collective_id=0, has_side_effects=True, vmem_limit_bytes=56 * 1024 * 1024
        ),
        cost_estimate=pl.CostEstimate(
            flops=4 * NR * COLS * E, bytes_accessed=4 * 1024 * 1024, transcendentals=3 * NR * COLS
        ),
        name="balanced_kmeans",
    )(stream, sample_index.reshape(ND // BLK, BLK), centroids)
    new_first = beta_one * first_moment + (1.0 - beta_one) * gradient
    new_second = beta_two * second_moment + (1.0 - beta_two) * gradient * gradient
    new_centroids = centroids - step_rate * new_first / (jnp.sqrt(new_second) + epsilon)
    return (new_centroids, new_first, new_second)


def solution(mesh):
    cut = P(("cent", "dp"), None)
    return jax.shard_map(
        per_device,
        mesh=mesh,
        in_specs=(P("dp", None), P("dp"), cut, cut, cut),
        out_specs=(cut, cut, cut),
        check_vma=False,
    )
```

```python
import functools
import math

import jax
import jax.numpy as jnp
from jax import lax
from jax.experimental import pallas as pl
from jax.experimental.pallas import tpu as pltpu
from jax.sharding import PartitionSpec as P

MESH = pl.DeviceIdType.MESH

KB = 16384
ROWS = 32768
NX, NY, NZ = 4, 4, 8
E = 768
OWN = 64
COLS = OWN * NZ
ND = 1024
BLK = 128
SLOTS = NY * ND // BLK
NR = SLOTS * BLK
STREAM = 2 * ND
BALANCE = math.log(ROWS / KB)
SUM_TYPE = jnp.bfloat16
HALF = E // 2

beta_one = 0.9
beta_two = 0.99
step_rate = 0.05
epsilon = 1e-08


def kernel(
    stream_hbm, idx, cent, grad,
    stream,    emb, piece, logits, transport, half_sq, col_part, col_part2, col_vec,
    row_vec, row_buf0, row_buf, row_sums, y_vec, y_buf0, y_buf, pot,
    col_send0, col_send, col_buf0, col_buf,
    partial, long_out, short_out, long_in, short_in,
    emb_send, emb_recv, sib_send, sib_recv, z_send, z_recv,
    row_send_sem, row_recv_sem, y_send_sem, y_recv_sem, col_send_sem, col_recv_sem,
    long_send_sem, long_recv_sem, short_send_sem, short_recv_sem, load_sem,
):
    dp = lax.axis_index("dp")
    group = lax.axis_index("cent")
    y, z = dp // NZ, lax.rem(dp, NZ)
    x, core = group // 2, lax.rem(group, 2)

    def at_y(k):
        return {"dp": lax.rem(y + k + NY, NY) * NZ + z, "cent": group}

    def at_z(k):
        return {"dp": y * NZ + lax.rem(z + k + NZ, NZ), "cent": group}

    def at_x(k):
        return {"dp": dp, "cent": lax.rem(x + k + NX, NX) * 2 + core}

    def at_group(k):
        return {"dp": dp, "cent": lax.rem(group + k, 2 * NX)}

    sibling = {"dp": dp, "cent": x * 2 + 1 - core}

    barrier = pltpu.get_barrier_semaphore()
    for device in (sibling, at_x(1), at_x(-1), at_y(1), at_y(-1), at_z(1), at_z(-1)):
        pl.semaphore_signal(barrier, inc=1, device_id=device, device_id_type=MESH)
    load = pltpu.make_async_copy(stream_hbm, stream, load_sem)
    load.start()

    pending = []

    def send(src, dst, send_sem, recv_sem, device):
        copy = pltpu.make_async_remote_copy(
            src_ref=src, dst_ref=dst, send_sem=send_sem, recv_sem=recv_sem,
            device_id=device, device_id_type=MESH,
        )
        copy.start()
        pending.append(copy)

    def arrived(dst, recv_sem):
        pltpu.make_async_remote_copy(
            src_ref=dst, dst_ref=dst, send_sem=recv_sem, recv_sem=recv_sem,
            device_id=sibling, device_id_type=MESH,
        ).wait_recv()

    def slot_of(k, c, j):
        return lax.rem(y + k + NY, NY) * 8 + c * 4 + lax.rem(x + j, 4)

    def emb_at(slot, count=1):
        return emb.at[pl.ds(pl.multiple_of(slot * BLK, BLK), count * BLK), :]

    sends = [0]

    def send_block(slot, device):
        send(emb_at(slot), emb_at(slot), emb_send.at[sends[0]], emb_recv.at[slot, 0], device)
        sends[0] += 1

    def wait_block(slot):
        arrived(emb_at(slot), emb_recv.at[slot, 0])

    def half_at(slot, h):
        return emb.at[pl.ds(pl.multiple_of(slot * BLK + h * (BLK // 2), BLK // 2), BLK // 2), :]

    def send_half(slot, h, device):
        send(half_at(slot, h), half_at(slot, h), emb_send.at[sends[0]], emb_recv.at[slot, h], device)
        sends[0] += 1

    def piece_at(k, h):
        owner = lax.rem(z + k + NZ, NZ)
        return piece.at[pl.ds(pl.multiple_of(owner * OWN + h * (OWN // 2), OWN // 2), OWN // 2), :]

    z_sends = [0]

    def send_piece(k, h, toward):
        owner = lax.rem(z + k + NZ, NZ)
        send(piece_at(k, h), piece_at(k, h), z_send.at[z_sends[0]], z_recv.at[owner, h], at_z(toward))
        z_sends[0] += 1

    def on_pieces(k, h, forward=True):
        for d in (-k, k):
            arrived(piece_at(d, h), z_recv.at[lax.rem(z + d + NZ, NZ), h])
            if forward or (d == -3):
                send_piece(d, h, 1 if d < 0 else -1)

    def gather(j):
        quarter = lax.rem(x + j, 4)
        picked = idx[pl.ds(core * 4 + quarter, 1), :].astype(jnp.float32)
        column = jnp.broadcast_to(picked, (BLK, BLK)).T[:, :1]
        place = lax.broadcasted_iota(jnp.int32, (BLK, STREAM), 1).astype(jnp.float32)
        one_hot = jnp.where(place == column, 1.0, 0.0).astype(jnp.bfloat16)
        rows = jnp.dot(one_hot, stream[...], preferred_element_type=jnp.float32)
        slot = slot_of(0, core, j)
        emb[pl.ds(pl.multiple_of(slot * BLK, BLK), BLK), :] = rows.astype(jnp.bfloat16)
        return slot

    piece[pl.ds(pl.multiple_of(z * OWN, OWN), OWN), :] = cent[...].astype(jnp.bfloat16)
    load.wait()
    first = gather(0)
    pl.semaphore_wait(barrier, 7)
    for h in (0, 1):
        send_piece(0, h, 1)
        send_piece(0, h, -1)
        send_half(first, h, at_y(1))
        send_half(first, h, at_y(-1))
    second = gather(2)
    gather(1)
    gather(3)
    own_first = y * 8 + core * 4
    send(emb_at(own_first, 4), emb_at(own_first, 4), sib_send, sib_recv, sibling)

    def on_half(k, j, h, forward=False, spread=False):
        slot = slot_of(k, core, j)
        arrived(half_at(slot, h), emb_recv.at[slot, h])
        if forward:
            send_half(slot, h, at_y(1))
        if spread:
            send_half(slot, h, at_x(1))
            send_half(slot, h, at_x(-1))
        if h:
            send_block(slot, sibling)

    def on_block(k, j, forward=False):
        slot = slot_of(k, core, j)
        wait_block(slot)
        if forward:
            send_block(slot, at_y(-1))
        send_block(slot, sibling)

    def score(blocks):
        starts = [pl.multiple_of(slot * BLK, BLK) for slot in blocks]
        rows = jnp.concatenate([emb[pl.ds(start, BLK), :] for start in starts], axis=0)
        product = lax.dot_general(
            piece[...], rows, (((1,), (1,)), ((), ())), preferred_element_type=jnp.float32
        )
        less = half_sq[...]
        for k, start in enumerate(starts):
            lanes = pl.ds(start, BLK)
            values = product[:, k * BLK:(k + 1) * BLK] - less
            logits[:, lanes] = values
            highest = jnp.max(values, axis=0, keepdims=True)
            row_vec[0:1, lanes] = highest
            row_vec[1:2, lanes] = jnp.sum(jnp.exp(values - highest), axis=0, keepdims=True)

    def score_from(offsets, c):
        blocks = [slot_of(k, c, j) for k, j in offsets]
        if offsets[0][0] and c is not core:
            for slot in blocks:
                wait_block(slot)
        score(blocks)

    own = [(0, 0), (0, 1), (0, 2), (0, 3)]
    early = [(-1, 0), (1, 0), (2, 0), (1, 2)]
    middle = [(-1, 1), (-1, 3), (1, 1), (1, 3)]
    late = [(-1, 2), (2, 2), (2, 1), (2, 3)]
    other = 1 - core

    on_pieces(1, 0)
    on_half(-1, 0, 0, forward=True, spread=True)
    on_half(1, 0, 0, spread=True)
    on_pieces(1, 1)
    on_half(-1, 0, 1, forward=True, spread=True)
    on_half(1, 0, 1, spread=True)
    send_block(second, at_y(1))
    send_block(second, at_y(-1))
    on_pieces(2, 0)
    on_pieces(2, 1)
    on_half(2, 0, 0, spread=True)
    on_pieces(3, 0, False)
    on_half(2, 0, 1, spread=True)
    on_pieces(3, 1, False)
    on_block(1, 2, forward=True)
    for h in (0, 1):
        on_half(-1, 1, h)
        on_half(-1, 3, h)
    for h in (0, 1):
        arrived(piece_at(-4, h), z_recv.at[lax.rem(z + 4, NZ), h])
    whole = piece[...].astype(jnp.float32)
    half_sq[...] = jnp.broadcast_to(
        0.5 * jnp.sum(whole * whole, axis=1, keepdims=True), (COLS, BLK)
    )
    score_from(own, core)
    score_from(early, core)
    arrived(emb_at(y * 8 + other * 4, 4), sib_recv)
    score_from(own, other)
    for h in (0, 1):
        on_half(1, 1, h)
        on_half(1, 3, h)
    on_block(-1, 2)
    score_from(early, other)
    score_from(middle, core)
    on_block(2, 2)
    for h in (0, 1):
        on_half(2, 1, h)
        on_half(2, 3, h)
    score_from(middle, other)
    score_from(late, core)
    score_from(late, other)

    def exchange_group(src, bufs, which):
        bufs[group] = src[...]
        for k in range(1, 2 * NX):
            send(
                src, bufs.at[group],
                row_send_sem.at[which, k - 1], row_recv_sem.at[which, group], at_group(k),
            )
        for k in range(1, 2 * NX):
            other = lax.rem(group + k, 2 * NX)
            arrived(bufs.at[other], row_recv_sem.at[which, other])

    def exchange_y(src, bufs, which):
        bufs[y] = src[...]
        for k in range(1, NY):
            send(
                src, bufs.at[y],
                y_send_sem.at[which, k - 1], y_recv_sem.at[which, y], at_y(k),
            )
        for k in range(1, NY):
            other = lax.rem(y + k, NY)
            arrived(bufs.at[other], y_recv_sem.at[which, other])

    def start_z(src, bufs, which):
        for k in range(1, NZ):
            send(
                src, bufs.at[z],
                col_send_sem.at[which, k - 1], col_recv_sem.at[which, z], at_z(k),
            )
        bufs[z] = src[...]

    def finish_z(bufs, which):
        for k in range(1, NZ):
            other = lax.rem(z + k, NZ)
            arrived(bufs.at[other], col_recv_sem.at[which, other])

    def exchange_z(src, bufs, which):
        start_z(src, bufs, which)
        finish_z(bufs, which)

    def merged(bufs, n):
        highest = bufs[0, 0:1, :]
        for k in range(1, n):
            highest = jnp.maximum(highest, bufs[k, 0:1, :])
        total = jnp.zeros_like(highest)
        for k in range(n):
            total = total + bufs[k, 1:2, :] * jnp.exp(bufs[k, 0:1, :] - highest)
        return highest, total

    def added(bufs, n):
        total = bufs[0]
        for k in range(1, n):
            total = total + bufs[k]
        return total

    def to_lanes(part):
        return jnp.transpose(part)

    def to_columns(vec):
        return jnp.transpose(jnp.broadcast_to(vec, (BLK, COLS)))

    exchange_group(row_vec, row_buf0, 0)
    highest, total = merged(row_buf0, 2 * NX)
    y_vec[0:1, :] = highest
    y_vec[1:2, :] = total
    exchange_y(y_vec, y_buf0, 0)
    highest, total = merged(y_buf0, NY)
    pot[...] = -(highest + jnp.log(total))

    def column_stats(g, carry):
        rows = pl.ds(pl.multiple_of(g * 16, 16), 16)
        tiles = [
            logits[rows, k * BLK:(k + 1) * BLK] + pot[:, k * BLK:(k + 1) * BLK] for k in range(SLOTS)
        ]
        highest = tiles[0]
        for tile in tiles[1:]:
            highest = jnp.maximum(highest, tile)
        total = jnp.exp(tiles[0] - highest)
        for tile in tiles[1:]:
            total = total + jnp.exp(tile - highest)
        col_part[rows, :] = highest
        col_part2[rows, :] = total
        return carry

    lax.fori_loop(0, COLS // 16, column_stats, 0)
    peaks = to_lanes(col_part[...])
    sums = to_lanes(col_part2[...])
    highest = jnp.max(peaks, axis=0, keepdims=True)
    col_send0[0:1, :] = highest
    col_send0[1:2, :] = jnp.sum(sums * jnp.exp(peaks - highest), axis=0, keepdims=True)
    exchange_z(col_send0, col_buf0, 0)
    highest, total = merged(col_buf0, NZ)
    col_vec[...] = to_columns(BALANCE - (highest + jnp.log(total)))

    WIDE = 2 * BLK

    def first_rows(t, carry):
        lanes = pl.ds(pl.multiple_of(t * WIDE, WIDE), WIDE)
        col = col_vec[...]
        both = jnp.concatenate([col, col], axis=1)
        plan = jnp.exp(logits[:, lanes] + pot[:, lanes] + both)
        logits[:, lanes] = plan
        row_sums[:, lanes] = jnp.sum(plan, axis=0, keepdims=True)
        return carry

    def later_rows(t, carry):
        lanes = pl.ds(pl.multiple_of(t * WIDE, WIDE), WIDE)
        col = col_vec[...]
        both = jnp.concatenate([col, col], axis=1)
        row_sums[:, lanes] = jnp.sum(logits[:, lanes] * both, axis=0, keepdims=True)
        return carry

    def row_factor(which):
        row_vec1 = row_buf.at[which - 1]
        y_bufs = y_buf.at[which - 1]
        src = row_src.at[which - 1]
        src[...] = row_sums[...]
        exchange_group(src, row_vec1, which)
        mid = y_src.at[which - 1]
        mid[...] = added(row_vec1, 2 * NX)
        exchange_y(mid, y_bufs, which)
        pot[...] = 1.0 / added(y_bufs, NY)

    row_src = row_buf.at[:, 2 * NX]
    y_src = y_buf.at[:, NY]

    def column_sums(g, carry):
        rows = pl.ds(pl.multiple_of(g * 32, 32), 32)
        total = logits[rows, 0:BLK] * pot[:, 0:BLK]
        for k in range(1, SLOTS):
            total = total + logits[rows, k * BLK:(k + 1) * BLK] * pot[:, k * BLK:(k + 1) * BLK]
        col_part[rows, :] = total
        return carry

    def start_total(which):
        src = col_send.at[which - 1]
        src[...] = jnp.sum(to_lanes(col_part[...]), axis=0, keepdims=True)
        start_z(src, col_buf.at[which - 1], which)

    def finish_total(which):
        finish_z(col_buf.at[which - 1], which)
        return added(col_buf.at[which - 1], NZ)

    lax.fori_loop(0, NR // WIDE, first_rows, 0)
    row_factor(1)
    for sweep in (1, 2):
        lax.fori_loop(0, COLS // 32, column_sums, 0)
        start_total(sweep)
        col_vec[...] = to_columns((ROWS / KB) / finish_total(sweep))
        lax.fori_loop(0, NR // WIDE, later_rows, 0)
        row_factor(sweep + 1)

    def make_transport(g, carry):
        rows = pl.ds(pl.multiple_of(g * 32, 32), 32)
        col = col_vec[rows, :]
        mass = jnp.zeros((32, BLK), jnp.float32)
        for k in range(SLOTS):
            lanes = slice(k * BLK, (k + 1) * BLK)
            rounded = (logits[rows, lanes] * pot[:, lanes] * col).astype(jnp.bfloat16)
            transport[rows, lanes] = rounded
            mass = mass + rounded.astype(jnp.float32)
        col_part[rows, :] = mass
        return carry

    lax.fori_loop(0, COLS // 32, make_transport, 0)

    def weigh(d0, d1):
        def rows_of(d):
            return transport[pl.ds(pl.multiple_of(lax.rem(z + d + NZ, NZ) * OWN, OWN), OWN), :]

        left = jnp.concatenate([rows_of(d0), rows_of(d1)], axis=0)

        def body(n, carry):
            lanes = pl.ds(pl.multiple_of(n * 256, 256), 256)
            both = jnp.dot(left, emb[:, lanes], preferred_element_type=jnp.float32)
            partial[d0 % NZ, :, lanes] = both[:OWN]
            partial[d1 % NZ, :, lanes] = both[OWN:]
            return carry

        lax.fori_loop(0, E // 256, body, 0)

    def features(h):
        return slice(h * HALF, (h + 1) * HALF)

    def long_step(h, s):
        way = 1 - 2 * h
        value = partial[(way * (4 - s)) % NZ, :, features(h)]
        if s:
            arrived(long_in.at[h * 4 + s - 1], long_recv_sem.at[h * 4 + s - 1])
            value = value + long_in[h * 4 + s - 1].astype(jnp.float32)
        at = h * 4 + s
        long_out[at] = value.astype(SUM_TYPE)
        send(long_out.at[at], long_in.at[at], long_send_sem.at[at], long_recv_sem.at[at], at_z(way))

    def short_step(h, s):
        way = 2 * h - 1
        value = partial[(way * (3 - s)) % NZ, :, features(h)]
        if s:
            arrived(short_in.at[h * 3 + s - 1], short_recv_sem.at[h * 3 + s - 1])
            value = value + short_in[h * 3 + s - 1].astype(jnp.float32)
        at = h * 3 + s
        short_out[at] = value.astype(SUM_TYPE)
        send(short_out.at[at], short_in.at[at], short_send_sem.at[at], short_recv_sem.at[at], at_z(way))

    start_total(3)
    weigh(4, 3)
    long_step(0, 0)
    long_step(1, 0)
    short_step(1, 0)
    weigh(-3, 2)
    short_step(0, 0)
    weigh(-2, 1)
    long_step(0, 1)
    long_step(1, 1)
    short_step(0, 1)
    short_step(1, 1)
    weigh(-1, 0)
    long_step(0, 2)
    long_step(1, 2)
    short_step(0, 2)
    short_step(1, 2)
    long_step(0, 3)
    long_step(1, 3)
    col_vec[...] = to_columns(finish_total(3))
    mass = col_vec[pl.ds(pl.multiple_of(z * OWN, OWN), OWN), :][:, :1]
    for h in (0, 1):
        arrived(short_in.at[h * 3 + 2], short_recv_sem.at[h * 3 + 2])
        weighted = partial[0, :, features(h)] + short_in[h * 3 + 2].astype(jnp.float32)
        arrived(long_in.at[h * 4 + 3], long_recv_sem.at[h * 4 + 3])
        weighted = weighted + long_in[h * 4 + 3].astype(jnp.float32)
        grad[:, features(h)] = (mass * cent[:, features(h)] - weighted) * (KB / ROWS)

    for copy in pending:
        copy.wait_send()


def per_device(stream, sample_index, centroids, first_moment, second_moment):
    f32 = jnp.float32
    scratch = [
        pltpu.VMEM((STREAM, E), jnp.bfloat16),
        pltpu.VMEM((NR, E), jnp.bfloat16),
        pltpu.VMEM((COLS, E), jnp.bfloat16),
        pltpu.VMEM((COLS, NR), f32),
        pltpu.VMEM((COLS, NR), jnp.bfloat16),
        pltpu.VMEM((COLS, BLK), f32),
        pltpu.VMEM((COLS, BLK), f32),
        pltpu.VMEM((COLS, BLK), f32),
        pltpu.VMEM((COLS, BLK), f32),
        pltpu.VMEM((2, NR), f32),
        pltpu.VMEM((2 * NX, 2, NR), f32),
        pltpu.VMEM((3, 2 * NX + 1, 1, NR), f32),
        pltpu.VMEM((1, NR), f32),
        pltpu.VMEM((2, NR), f32),
        pltpu.VMEM((NY, 2, NR), f32),
        pltpu.VMEM((3, NY + 1, 1, NR), f32),
        pltpu.VMEM((1, NR), f32),
        pltpu.VMEM((2, COLS), f32),
        pltpu.VMEM((3, 1, COLS), f32),
        pltpu.VMEM((NZ, 2, COLS), f32),
        pltpu.VMEM((3, NZ, 1, COLS), f32),
        pltpu.VMEM((NZ, OWN, E), f32),
        pltpu.VMEM((8, OWN, HALF), SUM_TYPE),
        pltpu.VMEM((6, OWN, HALF), SUM_TYPE),
        pltpu.VMEM((8, OWN, HALF), SUM_TYPE),
        pltpu.VMEM((6, OWN, HALF), SUM_TYPE),
        pltpu.SemaphoreType.DMA((40,)),
        pltpu.SemaphoreType.DMA((SLOTS, 2)),
        pltpu.SemaphoreType.DMA,
        pltpu.SemaphoreType.DMA,
        pltpu.SemaphoreType.DMA((14,)),
        pltpu.SemaphoreType.DMA((NZ, 2)),
        pltpu.SemaphoreType.DMA((4, 2 * NX - 1)),
        pltpu.SemaphoreType.DMA((4, 2 * NX)),
        pltpu.SemaphoreType.DMA((4, NY - 1)),
        pltpu.SemaphoreType.DMA((4, NY)),
        pltpu.SemaphoreType.DMA((4, NZ - 1)),
        pltpu.SemaphoreType.DMA((4, NZ)),
        pltpu.SemaphoreType.DMA((8,)),
        pltpu.SemaphoreType.DMA((8,)),
        pltpu.SemaphoreType.DMA((6,)),
        pltpu.SemaphoreType.DMA((6,)),
        pltpu.SemaphoreType.DMA,
    ]
    gradient = pl.pallas_call(
        kernel,
        out_shape=jax.ShapeDtypeStruct((OWN, E), f32),
        in_specs=[pl.BlockSpec(memory_space=pl.ANY)] + [pl.BlockSpec(memory_space=pltpu.VMEM)] * 2,
        out_specs=pl.BlockSpec(memory_space=pltpu.VMEM),
        scratch_shapes=scratch,
        compiler_params=pltpu.CompilerParams(
            collective_id=0, has_side_effects=True, vmem_limit_bytes=56 * 1024 * 1024
        ),
        cost_estimate=pl.CostEstimate(
            flops=4 * NR * COLS * E, bytes_accessed=4 * 1024 * 1024, transcendentals=3 * NR * COLS
        ),
        name="balanced_kmeans",
    )(stream, sample_index.reshape(ND // BLK, BLK), centroids)
    new_first = beta_one * first_moment + (1.0 - beta_one) * gradient
    new_second = beta_two * second_moment + (1.0 - beta_two) * gradient * gradient
    new_centroids = centroids - step_rate * new_first / (jnp.sqrt(new_second) + epsilon)
    return (new_centroids, new_first, new_second)


def solution(mesh):
    cut = P(("cent", "dp"), None)
    return jax.shard_map(
        per_device,
        mesh=mesh,
        in_specs=(P("dp", None), P("dp"), cut, cut, cut),
        out_specs=(cut, cut, cut),
        check_vma=False,
    )
```

```python
import functools
import math

import jax
import jax.numpy as jnp
from jax import lax
from jax.experimental import pallas as pl
from jax.experimental.pallas import tpu as pltpu
from jax.sharding import PartitionSpec as P

MESH = pl.DeviceIdType.MESH

KB = 16384
ROWS = 32768
NX, NY, NZ = 4, 4, 8
E = 768
OWN = 64
COLS = OWN * NZ
ND = 1024
BLK = 128
SLOTS = NY * ND // BLK
NR = SLOTS * BLK
STREAM = 2 * ND
BALANCE = math.log(ROWS / KB)
SUM_TYPE = jnp.bfloat16
CHUNK = 384
CHUNKS = E // CHUNK
PLANE = NX * NY

beta_one = 0.9
beta_two = 0.99
step_rate = 0.05
epsilon = 1e-08


def halving(op, parts):
    while len(parts) > 1:
        parts = [op(a, b) for a, b in zip(parts[::2], parts[1::2])]
    return parts[0]


def kernel(
    stream_hbm, idx, cent, grad,
    stream,    emb, piece, logits, transport, half_sq, col_part, col_part2, col_vec,
    row_own, row_sib, row_chip, row_plane, pot,
    col_send0, col_send, col_buf0, col_buf,
    partial, long_out, short_out, long_in, short_in,
    emb_send, emb_recv, sib_send, sib_recv, z_send, z_recv,
    row_sib_send, row_sib_recv, plane_send, plane_recv, col_send_sem, col_recv_sem,
    long_send_sem, long_recv_sem, short_send_sem, short_recv_sem, load_sem,
):
    dp = lax.axis_index("dp")
    group = lax.axis_index("cent")
    y, z = dp // NZ, lax.rem(dp, NZ)
    x, core = group // 2, lax.rem(group, 2)

    def at_y(k):
        return {"dp": lax.rem(y + k + NY, NY) * NZ + z, "cent": group}

    def at_z(k):
        return {"dp": y * NZ + lax.rem(z + k + NZ, NZ), "cent": group}

    def at_x(k):
        return {"dp": dp, "cent": lax.rem(x + k + NX, NX) * 2 + core}

    def at_plane(ky, kx):
        return {"dp": lax.rem(y + ky, NY) * NZ + z, "cent": lax.rem(x + kx, NX) * 2 + core}

    sibling = {"dp": dp, "cent": x * 2 + 1 - core}

    barrier = pltpu.get_barrier_semaphore()
    for device in (sibling, at_x(1), at_x(-1), at_y(1), at_y(-1), at_z(1), at_z(-1)):
        pl.semaphore_signal(barrier, inc=1, device_id=device, device_id_type=MESH)
    load = pltpu.make_async_copy(stream_hbm, stream, load_sem)
    load.start()

    pending = []

    def send(src, dst, send_sem, recv_sem, device):
        copy = pltpu.make_async_remote_copy(
            src_ref=src, dst_ref=dst, send_sem=send_sem, recv_sem=recv_sem,
            device_id=device, device_id_type=MESH,
        )
        copy.start()
        pending.append(copy)

    def arrived(dst, recv_sem):
        pltpu.make_async_remote_copy(
            src_ref=dst, dst_ref=dst, send_sem=recv_sem, recv_sem=recv_sem,
            device_id=sibling, device_id_type=MESH,
        ).wait_recv()

    def slot_of(k, c, j):
        return lax.rem(y + k + NY, NY) * 8 + c * 4 + lax.rem(x + j, 4)

    def emb_at(slot, count=1):
        return emb.at[pl.ds(pl.multiple_of(slot * BLK, BLK), count * BLK), :]

    sends = [0]

    def send_block(slot, device):
        send(emb_at(slot), emb_at(slot), emb_send.at[sends[0]], emb_recv.at[slot, 0], device)
        sends[0] += 1

    def wait_block(slot):
        arrived(emb_at(slot), emb_recv.at[slot, 0])

    def half_at(slot, h):
        return emb.at[pl.ds(pl.multiple_of(slot * BLK + h * (BLK // 2), BLK // 2), BLK // 2), :]

    def send_half(slot, h, device):
        send(half_at(slot, h), half_at(slot, h), emb_send.at[sends[0]], emb_recv.at[slot, h], device)
        sends[0] += 1

    def piece_at(k, h):
        owner = lax.rem(z + k + NZ, NZ)
        return piece.at[pl.ds(pl.multiple_of(owner * OWN + h * (OWN // 2), OWN // 2), OWN // 2), :]

    z_sends = [0]

    def send_piece(k, h, toward):
        owner = lax.rem(z + k + NZ, NZ)
        send(piece_at(k, h), piece_at(k, h), z_send.at[z_sends[0]], z_recv.at[owner, h], at_z(toward))
        z_sends[0] += 1

    def on_pieces(k, h, forward=True):
        for d in (-k, k):
            arrived(piece_at(d, h), z_recv.at[lax.rem(z + d + NZ, NZ), h])
            if forward or (d == -3):
                send_piece(d, h, 1 if d < 0 else -1)

    def gather(j):
        quarter = lax.rem(x + j, 4)
        picked = idx[pl.ds(core * 4 + quarter, 1), :].astype(jnp.float32)
        column = jnp.broadcast_to(picked, (BLK, BLK)).T[:, :1]
        place = lax.broadcasted_iota(jnp.int32, (BLK, STREAM), 1).astype(jnp.float32)
        one_hot = jnp.where(place == column, 1.0, 0.0).astype(jnp.bfloat16)
        rows = jnp.dot(one_hot, stream[...], preferred_element_type=jnp.float32)
        slot = slot_of(0, core, j)
        emb[pl.ds(pl.multiple_of(slot * BLK, BLK), BLK), :] = rows.astype(jnp.bfloat16)
        return slot

    piece[pl.ds(pl.multiple_of(z * OWN, OWN), OWN), :] = cent[...].astype(jnp.bfloat16)
    pl.semaphore_wait(barrier, 7)
    for h in (0, 1):
        send_piece(0, h, 1)
        send_piece(0, h, -1)
    load.wait()
    first = gather(0)
    for h in (0, 1):
        send_half(first, h, at_y(1))
        send_half(first, h, at_y(-1))
    second = gather(2)
    gather(1)
    gather(3)
    own_first = y * 8 + core * 4
    send(emb_at(own_first, 4), emb_at(own_first, 4), sib_send, sib_recv, sibling)

    def on_half(k, j, h, forward=False, spread=False):
        slot = slot_of(k, core, j)
        arrived(half_at(slot, h), emb_recv.at[slot, h])
        if forward:
            send_half(slot, h, at_y(1))
        if spread:
            send_half(slot, h, at_x(1))
            send_half(slot, h, at_x(-1))
        if j:
            send_half(slot, h, sibling)
        elif h:
            send_block(slot, sibling)

    def on_block(k, j, forward=False):
        slot = slot_of(k, core, j)
        wait_block(slot)
        if forward:
            send_block(slot, at_y(-1))
        send_block(slot, sibling)

    def score(blocks):
        starts = [pl.multiple_of(slot * BLK, BLK) for slot in blocks]
        rows = jnp.concatenate([emb[pl.ds(start, BLK), :] for start in starts], axis=0)
        product = lax.dot_general(
            piece[...], rows, (((1,), (1,)), ((), ())), preferred_element_type=jnp.float32
        )
        less = half_sq[...]
        for k, start in enumerate(starts):
            lanes = pl.ds(start, BLK)
            values = product[:, k * BLK:(k + 1) * BLK] - less
            logits[:, lanes] = values
            highest = jnp.max(values, axis=0, keepdims=True)
            total = jnp.sum(jnp.exp(values - highest), axis=0, keepdims=True)
            row_own[0, pl.ds(blocks[k], 1), :] = highest + jnp.log(total)

    def score_from(offsets, c):
        blocks = [slot_of(k, c, j) for k, j in offsets]
        if offsets[0][0] and c is not core:
            for (_, j), slot in zip(offsets, blocks):
                if j % 2:
                    for h in (0, 1):
                        arrived(half_at(slot, h), emb_recv.at[slot, h])
                else:
                    wait_block(slot)
        score(blocks)

    own = [(0, 0), (0, 1), (0, 2), (0, 3)]
    early = [(-1, 0), (1, 0), (2, 0), (1, 2)]
    middle = [(-1, 1), (-1, 3), (1, 1), (1, 3)]
    late = [(-1, 2), (2, 2), (2, 1), (2, 3)]
    other = 1 - core

    on_pieces(1, 0)
    on_half(-1, 0, 0, forward=True, spread=True)
    on_half(1, 0, 0, spread=True)
    on_pieces(1, 1)
    on_half(-1, 0, 1, forward=True, spread=True)
    on_half(1, 0, 1, spread=True)
    send_block(second, at_y(1))
    send_block(second, at_y(-1))
    on_pieces(2, 0)
    on_pieces(2, 1)
    on_half(2, 0, 0, spread=True)
    on_pieces(3, 0, False)
    on_half(2, 0, 1, spread=True)
    on_pieces(3, 1, False)
    on_block(1, 2, forward=True)
    for h in (0, 1):
        on_half(-1, 1, h)
        on_half(-1, 3, h)
    for h in (0, 1):
        arrived(piece_at(-4, h), z_recv.at[lax.rem(z + 4, NZ), h])
    whole = piece[...].astype(jnp.float32)
    half_sq[...] = jnp.broadcast_to(
        0.5 * jnp.sum(whole * whole, axis=1, keepdims=True), (COLS, BLK)
    )
    score_from(own, core)
    score_from(early, core)
    arrived(emb_at(y * 8 + other * 4, 4), sib_recv)
    score_from(own, other)
    for h in (0, 1):
        on_half(1, 1, h)
        on_half(1, 3, h)
    on_block(-1, 2)
    score_from(early, other)
    score_from(middle, core)
    on_block(2, 2)
    for h in (0, 1):
        on_half(2, 1, h)
        on_half(2, 3, h)
    score_from(middle, other)
    score_from(late, core)
    score_from(late, other)

    plane_peers = [(ky, kx) for ky in (2, 1, 3, 0) for kx in (2, 1, 3, 0) if ky or kx]

    def exchange_rows(p, combine):
        send(row_own.at[p], row_sib.at[p], row_sib_send.at[p], row_sib_recv.at[p], sibling)
        arrived(row_sib.at[p], row_sib_recv.at[p])
        chip = combine([row_own[p], row_sib[p]])
        row_chip[p] = chip
        me = y * NX + x
        for at, (ky, kx) in enumerate(plane_peers):
            send(row_chip.at[p], row_plane.at[p, me], plane_send.at[p, at], plane_recv.at[p, me], at_plane(ky, kx))
        row_plane[p, me] = chip
        for ky, kx in reversed(plane_peers):
            peer = lax.rem(y + ky, NY) * NX + lax.rem(x + kx, NX)
            arrived(row_plane.at[p, peer], plane_recv.at[p, peer])
        return combine([row_plane[p, k] for k in range(PLANE)])

    def log_sum(parts):
        highest = functools.reduce(jnp.maximum, parts)
        total = functools.reduce(jnp.add, [jnp.exp(part - highest) for part in parts])
        return highest + jnp.log(total)

    def plain_sum(parts):
        return functools.reduce(jnp.add, parts)

    def start_z(src, bufs, which):
        for k in range(1, NZ):
            send(
                src, bufs.at[z],
                col_send_sem.at[which, k - 1], col_recv_sem.at[which, z], at_z(k),
            )
        bufs[z] = src[...]

    def finish_z(bufs, which):
        for k in range(1, NZ):
            other = lax.rem(z + k, NZ)
            arrived(bufs.at[other], col_recv_sem.at[which, other])

    def exchange_z(src, bufs, which):
        start_z(src, bufs, which)
        finish_z(bufs, which)

    def merged(bufs, n):
        highest = bufs[0, 0:1, :]
        for k in range(1, n):
            highest = jnp.maximum(highest, bufs[k, 0:1, :])
        total = jnp.zeros_like(highest)
        for k in range(n):
            total = total + bufs[k, 1:2, :] * jnp.exp(bufs[k, 0:1, :] - highest)
        return highest, total

    def added(bufs, n):
        total = bufs[0]
        for k in range(1, n):
            total = total + bufs[k]
        return total

    def to_lanes(part):
        return jnp.transpose(part)

    def to_columns(vec):
        return jnp.transpose(jnp.broadcast_to(vec, (BLK, COLS)))

    pot[...] = -exchange_rows(0, log_sum)

    def column_stats(g, carry):
        rows = pl.ds(pl.multiple_of(g * 16, 16), 16)
        tiles = [
            logits[rows, k * BLK:(k + 1) * BLK] + pot[k:k + 1, :] for k in range(SLOTS)
        ]
        highest = halving(jnp.maximum, tiles)
        col_part[rows, :] = highest
        col_part2[rows, :] = halving(jnp.add, [jnp.exp(tile - highest) for tile in tiles])
        return carry

    lax.fori_loop(0, COLS // 16, column_stats, 0)
    peaks = to_lanes(col_part[...])
    sums = to_lanes(col_part2[...])
    highest = jnp.max(peaks, axis=0, keepdims=True)
    col_send0[0:1, :] = highest
    col_send0[1:2, :] = jnp.sum(sums * jnp.exp(peaks - highest), axis=0, keepdims=True)
    exchange_z(col_send0, col_buf0, 0)
    highest, total = merged(col_buf0, NZ)
    col_vec[...] = to_columns(BALANCE - (highest + jnp.log(total)))

    def lanes_of(t):
        return pl.ds(pl.multiple_of(t * 4 * BLK, 4 * BLK), 4 * BLK)

    def keep_sums(p, t, values):
        sums = jnp.sum(values, axis=0, keepdims=True)
        for u in range(4):
            row_own[p, pl.ds(4 * t + u, 1), :] = sums[:, u * BLK:(u + 1) * BLK]

    def first_rows(t, carry):
        row = jnp.concatenate([pot[pl.ds(4 * t + u, 1), :] for u in range(4)], axis=1)
        plan = jnp.exp(logits[:, lanes_of(t)] + row + jnp.concatenate([col_vec[...]] * 4, axis=1))
        logits[:, lanes_of(t)] = plan
        keep_sums(1, t, plan)
        return carry

    def later_rows(p):
        def body(t, carry):
            keep_sums(p, t, logits[:, lanes_of(t)] * jnp.concatenate([col_vec[...]] * 4, axis=1))
            return carry

        lax.fori_loop(0, SLOTS // 4, body, 0)

    def column_sums(g, carry):
        rows = pl.ds(pl.multiple_of(g * 64, 64), 64)
        total = logits[rows, 0:BLK] * pot[0:1, :]
        for k in range(1, SLOTS):
            total = total + logits[rows, k * BLK:(k + 1) * BLK] * pot[k:k + 1, :]
        col_part[rows, :] = total
        return carry

    def start_total(which):
        src = col_send.at[which - 1]
        src[...] = jnp.sum(to_lanes(col_part[...]), axis=0, keepdims=True)
        start_z(src, col_buf.at[which - 1], which)

    def finish_total(which):
        finish_z(col_buf.at[which - 1], which)
        return added(col_buf.at[which - 1], NZ)

    lax.fori_loop(0, SLOTS // 4, first_rows, 0)
    pot[...] = 1.0 / exchange_rows(1, plain_sum)
    for sweep in (1, 2):
        lax.fori_loop(0, COLS // 64, column_sums, 0)
        start_total(sweep)
        col_vec[...] = to_columns((ROWS / KB) / finish_total(sweep))
        later_rows(sweep + 1)
        pot[...] = 1.0 / exchange_rows(sweep + 1, plain_sum)

    def make_transport(d):
        def body(g, carry):
            start = lax.rem(z + d + NZ, NZ) * OWN + g * 32
            rows = pl.ds(pl.multiple_of(start, 32), 32)
            col = col_vec[rows, :]
            mass = jnp.zeros((32, BLK), jnp.float32)
            for k in range(SLOTS):
                lanes = slice(k * BLK, (k + 1) * BLK)
                rounded = (logits[rows, lanes] * pot[k:k + 1, :] * col).astype(jnp.bfloat16)
                transport[rows, lanes] = rounded
                mass = mass + rounded.astype(jnp.float32)
            col_part[rows, :] = mass
            return carry

        lax.fori_loop(0, OWN // 32, body, 0)

    def weigh(d0, d1, n):
        def rows_of(d):
            return transport[pl.ds(pl.multiple_of(lax.rem(z + d + NZ, NZ) * OWN, OWN), OWN), :]

        left = jnp.concatenate([rows_of(d0), rows_of(d1)], axis=0)
        lanes = slice(n * 2 * CHUNK, (n + 1) * 2 * CHUNK)
        both = jnp.dot(left, emb[:, lanes], preferred_element_type=jnp.float32)
        partial[d0 % NZ, :, lanes] = both[:OWN]
        partial[d1 % NZ, :, lanes] = both[OWN:]

    def features(h):
        return slice(h * CHUNK, (h + 1) * CHUNK)

    def long_step(h, s):
        way = 1 - 2 * (h % 2)
        value = partial[(way * (4 - s)) % NZ, :, features(h)]
        if s:
            arrived(long_in.at[h * 4 + s - 1], long_recv_sem.at[h * 4 + s - 1])
            value = value + long_in[h * 4 + s - 1].astype(jnp.float32)
        at = h * 4 + s
        long_out[at] = value.astype(SUM_TYPE)
        send(long_out.at[at], long_in.at[at], long_send_sem.at[at], long_recv_sem.at[at], at_z(way))

    def short_step(h, s):
        way = 2 * (h % 2) - 1
        value = partial[(way * (3 - s)) % NZ, :, features(h)]
        if s:
            arrived(short_in.at[h * 3 + s - 1], short_recv_sem.at[h * 3 + s - 1])
            value = value + short_in[h * 3 + s - 1].astype(jnp.float32)
        at = h * 3 + s
        short_out[at] = value.astype(SUM_TYPE)
        send(short_out.at[at], short_in.at[at], short_send_sem.at[at], short_recv_sem.at[at], at_z(way))

    make_transport(4)
    make_transport(3)
    for n in range(CHUNKS // 2):
        weigh(4, 3, n)
        for h in (2 * n, 2 * n + 1):
            long_step(h, 0)
        short_step(2 * n + 1, 0)
    make_transport(-3)
    make_transport(2)
    for n in range(CHUNKS // 2):
        weigh(-3, 2, n)
        short_step(2 * n, 0)
    for h in range(CHUNKS):
        long_step(h, 1)
        if h % 2:
            short_step(h, 1)
    make_transport(-2)
    make_transport(1)
    for n in range(CHUNKS // 2):
        weigh(-2, 1, n)
    for n in range(CHUNKS // 2):
        short_step(2 * n, 1)
        for h in (2 * n, 2 * n + 1):
            long_step(h, 2)
        short_step(2 * n + 1, 2)
    make_transport(-1)
    make_transport(0)
    start_total(3)
    for n in range(CHUNKS // 2):
        weigh(-1, 0, n)
        short_step(2 * n, 2)
    for h in range(CHUNKS):
        long_step(h, 3)
    col_vec[...] = to_columns(finish_total(3))
    mass = col_vec[pl.ds(pl.multiple_of(z * OWN, OWN), OWN), :][:, :1]
    for h in range(CHUNKS):
        arrived(short_in.at[h * 3 + 2], short_recv_sem.at[h * 3 + 2])
        weighted = partial[0, :, features(h)] + short_in[h * 3 + 2].astype(jnp.float32)
        arrived(long_in.at[h * 4 + 3], long_recv_sem.at[h * 4 + 3])
        weighted = weighted + long_in[h * 4 + 3].astype(jnp.float32)
        grad[:, features(h)] = (mass * cent[:, features(h)] - weighted) * (KB / ROWS)

    for copy in pending:
        copy.wait_send()


def per_device(stream, sample_index, centroids, first_moment, second_moment):
    f32 = jnp.float32
    scratch = [
        pltpu.VMEM((STREAM, E), jnp.bfloat16),
        pltpu.VMEM((NR, E), jnp.bfloat16),
        pltpu.VMEM((COLS, E), jnp.bfloat16),
        pltpu.VMEM((COLS, NR), f32),
        pltpu.VMEM((COLS, NR), jnp.bfloat16),
        pltpu.VMEM((COLS, BLK), f32),
        pltpu.VMEM((COLS, BLK), f32),
        pltpu.VMEM((COLS, BLK), f32),
        pltpu.VMEM((COLS, BLK), f32),
        pltpu.VMEM((4, SLOTS, BLK), f32),
        pltpu.VMEM((4, SLOTS, BLK), f32),
        pltpu.VMEM((4, SLOTS, BLK), f32),
        pltpu.VMEM((4, PLANE, SLOTS, BLK), f32),
        pltpu.VMEM((SLOTS, BLK), f32),
        pltpu.VMEM((2, COLS), f32),
        pltpu.VMEM((3, 1, COLS), f32),
        pltpu.VMEM((NZ, 2, COLS), f32),
        pltpu.VMEM((3, NZ, 1, COLS), f32),
        pltpu.VMEM((NZ, OWN, E), f32),
        pltpu.VMEM((4 * CHUNKS, OWN, CHUNK), SUM_TYPE),
        pltpu.VMEM((3 * CHUNKS, OWN, CHUNK), SUM_TYPE),
        pltpu.VMEM((4 * CHUNKS, OWN, CHUNK), SUM_TYPE),
        pltpu.VMEM((3 * CHUNKS, OWN, CHUNK), SUM_TYPE),
        pltpu.SemaphoreType.DMA((40,)),
        pltpu.SemaphoreType.DMA((SLOTS, 2)),
        pltpu.SemaphoreType.DMA,
        pltpu.SemaphoreType.DMA,
        pltpu.SemaphoreType.DMA((14,)),
        pltpu.SemaphoreType.DMA((NZ, 2)),
        pltpu.SemaphoreType.DMA((4,)),
        pltpu.SemaphoreType.DMA((4,)),
        pltpu.SemaphoreType.DMA((4, PLANE - 1)),
        pltpu.SemaphoreType.DMA((4, PLANE)),
        pltpu.SemaphoreType.DMA((4, NZ - 1)),
        pltpu.SemaphoreType.DMA((4, NZ)),
        pltpu.SemaphoreType.DMA((4 * CHUNKS,)),
        pltpu.SemaphoreType.DMA((4 * CHUNKS,)),
        pltpu.SemaphoreType.DMA((3 * CHUNKS,)),
        pltpu.SemaphoreType.DMA((3 * CHUNKS,)),
        pltpu.SemaphoreType.DMA,
    ]
    gradient = pl.pallas_call(
        kernel,
        out_shape=jax.ShapeDtypeStruct((OWN, E), f32),
        in_specs=[pl.BlockSpec(memory_space=pl.ANY)] + [pl.BlockSpec(memory_space=pltpu.VMEM)] * 2,
        out_specs=pl.BlockSpec(memory_space=pltpu.VMEM),
        scratch_shapes=scratch,
        compiler_params=pltpu.CompilerParams(
            collective_id=0, has_side_effects=True, vmem_limit_bytes=56 * 1024 * 1024
        ),
        cost_estimate=pl.CostEstimate(
            flops=4 * NR * COLS * E, bytes_accessed=4 * 1024 * 1024, transcendentals=3 * NR * COLS
        ),
        name="balanced_kmeans",
    )(stream, sample_index.reshape(ND // BLK, BLK), centroids)
    new_first = beta_one * first_moment + (1.0 - beta_one) * gradient
    new_second = beta_two * second_moment + (1.0 - beta_two) * gradient * gradient
    new_centroids = centroids - step_rate * new_first / (jnp.sqrt(new_second) + epsilon)
    return (new_centroids, new_first, new_second)


def solution(mesh):
    cut = P(("cent", "dp"), None)
    return jax.shard_map(
        per_device,
        mesh=mesh,
        in_specs=(P("dp", None), P("dp"), cut, cut, cut),
        out_specs=(cut, cut, cut),
        check_vma=False,
    )
```

```python
import functools
import math

import jax
import jax.numpy as jnp
from jax import lax
from jax.experimental import pallas as pl
from jax.experimental.pallas import tpu as pltpu
from jax.sharding import PartitionSpec as P

MESH = pl.DeviceIdType.MESH

KB = 16384
ROWS = 32768
NX, NY, NZ = 4, 4, 8
E = 768
OWN = 64
COLS = OWN * NZ
ND = 1024
BLK = 128
PARTS = 2
SLOTS = NY * ND // BLK
NR = SLOTS * BLK
STREAM = 2 * ND
BALANCE = math.log(ROWS / KB)
SUM_TYPE = jnp.bfloat16
CHUNK = 384
CHUNKS = E // CHUNK
PLANE = NX * NY

beta_one = 0.9
beta_two = 0.99
step_rate = 0.05
epsilon = 1e-08


def halving(op, parts):
    while len(parts) > 1:
        parts = [op(a, b) for a, b in zip(parts[::2], parts[1::2])]
    return parts[0]


def kernel(
    stream_hbm, idx, cent, grad,
    stream,    emb, piece, logits, transport, half_sq, col_part, col_part2, col_vec,
    row_own, row_sib, row_chip, row_plane, pot,
    col_send0, col_send, col_buf0, col_buf,
    partial, long_out, short_out, long_in, short_in,
    emb_send, emb_recv, sib_send, sib_recv, z_send, z_recv,
    row_sib_send, row_sib_recv, plane_send, plane_recv, col_send_sem, col_recv_sem,
    long_send_sem, long_recv_sem, short_send_sem, short_recv_sem, load_sem,
):
    dp = lax.axis_index("dp")
    group = lax.axis_index("cent")
    y, z = dp // NZ, lax.rem(dp, NZ)
    x, core = group // 2, lax.rem(group, 2)

    def at_y(k):
        return {"dp": lax.rem(y + k + NY, NY) * NZ + z, "cent": group}

    def at_z(k):
        return {"dp": y * NZ + lax.rem(z + k + NZ, NZ), "cent": group}

    def at_x(k):
        return {"dp": dp, "cent": lax.rem(x + k + NX, NX) * 2 + core}

    def at_plane(ky, kx):
        return {"dp": lax.rem(y + ky, NY) * NZ + z, "cent": lax.rem(x + kx, NX) * 2 + core}

    sibling = {"dp": dp, "cent": x * 2 + 1 - core}

    barrier = pltpu.get_barrier_semaphore()
    for device in (sibling, at_x(1), at_x(-1), at_y(1), at_y(-1), at_z(1), at_z(-1)):
        pl.semaphore_signal(barrier, inc=1, device_id=device, device_id_type=MESH)
    load = pltpu.make_async_copy(stream_hbm, stream, load_sem)
    load.start()

    pending = []

    def send(src, dst, send_sem, recv_sem, device):
        copy = pltpu.make_async_remote_copy(
            src_ref=src, dst_ref=dst, send_sem=send_sem, recv_sem=recv_sem,
            device_id=device, device_id_type=MESH,
        )
        copy.start()
        pending.append(copy)

    def arrived(dst, recv_sem):
        pltpu.make_async_remote_copy(
            src_ref=dst, dst_ref=dst, send_sem=recv_sem, recv_sem=recv_sem,
            device_id=sibling, device_id_type=MESH,
        ).wait_recv()

    def slot_of(k, c, j):
        return lax.rem(y + k + NY, NY) * 8 + c * 4 + lax.rem(x + j, 4)

    def emb_at(slot, count=1):
        return emb.at[pl.ds(pl.multiple_of(slot * BLK, BLK), count * BLK), :]

    sends = [0]

    def send_block(slot, device):
        send(emb_at(slot), emb_at(slot), emb_send.at[sends[0]], emb_recv.at[slot, 0], device)
        sends[0] += 1

    def wait_block(slot):
        arrived(emb_at(slot), emb_recv.at[slot, 0])

    def part_at(slot, h):
        return emb.at[pl.ds(pl.multiple_of(slot * BLK + h * (BLK // PARTS), BLK // PARTS), BLK // PARTS), :]

    def send_part(slot, h, device):
        send(part_at(slot, h), part_at(slot, h), emb_send.at[sends[0]], emb_recv.at[slot, h], device)
        sends[0] += 1

    def piece_at(k, h):
        owner = lax.rem(z + k + NZ, NZ)
        return piece.at[pl.ds(pl.multiple_of(owner * OWN + h * (OWN // 2), OWN // 2), OWN // 2), :]

    z_sends = [0]

    def send_piece(k, h, toward):
        owner = lax.rem(z + k + NZ, NZ)
        send(piece_at(k, h), piece_at(k, h), z_send.at[z_sends[0]], z_recv.at[owner, h], at_z(toward))
        z_sends[0] += 1

    def on_pieces(k, h, forward=True):
        for d in (-k, k):
            arrived(piece_at(d, h), z_recv.at[lax.rem(z + d + NZ, NZ), h])
            if forward or (d == -3):
                send_piece(d, h, 1 if d < 0 else -1)

    def gather(j):
        quarter = lax.rem(x + j, 4)
        picked = idx[pl.ds(core * 4 + quarter, 1), :].astype(jnp.float32)
        column = jnp.broadcast_to(picked, (BLK, BLK)).T[:, :1]
        place = lax.broadcasted_iota(jnp.int32, (BLK, STREAM), 1).astype(jnp.float32)
        one_hot = jnp.where(place == column, 1.0, 0.0).astype(jnp.bfloat16)
        rows = jnp.dot(one_hot, stream[...], preferred_element_type=jnp.float32)
        slot = slot_of(0, core, j)
        emb[pl.ds(pl.multiple_of(slot * BLK, BLK), BLK), :] = rows.astype(jnp.bfloat16)
        return slot

    piece[pl.ds(pl.multiple_of(z * OWN, OWN), OWN), :] = cent[...].astype(jnp.bfloat16)
    load.wait()
    first = gather(0)
    pl.semaphore_wait(barrier, 7)
    for h in range(PARTS):
        send_part(first, h, at_y(1))
        send_part(first, h, at_y(-1))
    for h in (0, 1):
        send_piece(0, h, 1)
        send_piece(0, h, -1)
    second = gather(2)
    gather(1)
    gather(3)
    own_first = y * 8 + core * 4
    send(emb_at(own_first, 4), emb_at(own_first, 4), sib_send, sib_recv, sibling)

    def on_part(k, j, h, forward=False, spread=False):
        slot = slot_of(k, core, j)
        arrived(part_at(slot, h), emb_recv.at[slot, h])
        if forward:
            send_part(slot, h, at_y(1))
        if spread:
            send_part(slot, h, at_x(1))
            send_part(slot, h, at_x(-1))
        if h == PARTS - 1:
            send_block(slot, sibling)

    def on_block(k, j, forward=False):
        slot = slot_of(k, core, j)
        wait_block(slot)
        if forward:
            send_block(slot, at_y(-1))
        send_block(slot, sibling)

    def score(blocks):
        starts = [pl.multiple_of(slot * BLK, BLK) for slot in blocks]
        rows = jnp.concatenate([emb[pl.ds(start, BLK), :] for start in starts], axis=0)
        product = lax.dot_general(
            piece[...], rows, (((1,), (1,)), ((), ())), preferred_element_type=jnp.float32
        )
        less = half_sq[...]
        for k, start in enumerate(starts):
            lanes = pl.ds(start, BLK)
            values = product[:, k * BLK:(k + 1) * BLK] - less
            logits[:, lanes] = values
            highest = jnp.max(values, axis=0, keepdims=True)
            total = jnp.sum(jnp.exp(values - highest), axis=0, keepdims=True)
            row_own[0, pl.ds(blocks[k], 1), :] = highest + jnp.log(total)

    def score_from(offsets, c):
        blocks = [slot_of(k, c, j) for k, j in offsets]
        if offsets[0][0] and c is not core:
            for slot in blocks:
                wait_block(slot)
        score(blocks)

    own = [(0, 0), (0, 1), (0, 2), (0, 3)]
    early = [(-1, 0), (1, 0), (2, 0), (1, 2)]
    middle = [(-1, 1), (-1, 3), (1, 1), (1, 3)]
    late = [(-1, 2), (2, 2), (2, 1), (2, 3)]
    other = 1 - core

    on_pieces(1, 0)
    for h in range(PARTS):
        on_part(-1, 0, h, forward=True, spread=True)
        on_part(1, 0, h, spread=True)
        if h == PARTS // 2 - 1:
            on_pieces(1, 1)
            send_block(second, at_y(-1))
    send_block(second, at_y(1))
    on_pieces(2, 0)
    on_pieces(2, 1)
    for h in range(PARTS):
        on_part(2, 0, h, spread=True)
        if h == PARTS // 2 - 1:
            on_pieces(3, 0, False)
    on_pieces(3, 1, False)
    on_block(1, 2, forward=True)
    for h in range(PARTS):
        on_part(-1, 1, h)
        on_part(-1, 3, h)
    for h in (0, 1):
        arrived(piece_at(-4, h), z_recv.at[lax.rem(z + 4, NZ), h])
    whole = piece[...].astype(jnp.float32)
    half_sq[...] = jnp.broadcast_to(
        0.5 * jnp.sum(whole * whole, axis=1, keepdims=True), (COLS, BLK)
    )
    score_from(own, core)
    score_from(early, core)
    arrived(emb_at(y * 8 + other * 4, 4), sib_recv)
    score_from(own, other)
    for h in range(PARTS):
        on_part(1, 1, h)
        on_part(1, 3, h)
    on_block(-1, 2)
    score_from(early, other)
    score_from(middle, core)
    on_block(2, 2)
    for h in range(PARTS):
        on_part(2, 1, h)
        on_part(2, 3, h)
    score_from(middle, other)
    score_from(late, core)
    score_from(late, other)

    plane_peers = [(ky, kx) for ky in (2, 1, 3, 0) for kx in (2, 1, 3, 0) if ky or kx]

    def exchange_rows(p, combine):
        send(row_own.at[p], row_sib.at[p], row_sib_send.at[p], row_sib_recv.at[p], sibling)
        arrived(row_sib.at[p], row_sib_recv.at[p])
        chip = combine([row_own[p], row_sib[p]])
        row_chip[p] = chip
        me = y * NX + x
        for at, (ky, kx) in enumerate(plane_peers):
            send(row_chip.at[p], row_plane.at[p, me], plane_send.at[p, at], plane_recv.at[p, me], at_plane(ky, kx))
        row_plane[p, me] = chip
        for ky, kx in reversed(plane_peers):
            peer = lax.rem(y + ky, NY) * NX + lax.rem(x + kx, NX)
            arrived(row_plane.at[p, peer], plane_recv.at[p, peer])
        return combine([row_plane[p, k] for k in range(PLANE)])

    def log_sum(parts):
        highest = functools.reduce(jnp.maximum, parts)
        total = functools.reduce(jnp.add, [jnp.exp(part - highest) for part in parts])
        return highest + jnp.log(total)

    def plain_sum(parts):
        return functools.reduce(jnp.add, parts)

    def start_z(src, bufs, which):
        for k in range(1, NZ):
            send(
                src, bufs.at[z],
                col_send_sem.at[which, k - 1], col_recv_sem.at[which, z], at_z(k),
            )
        bufs[z] = src[...]

    def finish_z(bufs, which):
        for k in range(1, NZ):
            other = lax.rem(z + k, NZ)
            arrived(bufs.at[other], col_recv_sem.at[which, other])

    def exchange_z(src, bufs, which):
        start_z(src, bufs, which)
        finish_z(bufs, which)

    def merged(bufs, n):
        highest = bufs[0, 0:1, :]
        for k in range(1, n):
            highest = jnp.maximum(highest, bufs[k, 0:1, :])
        total = jnp.zeros_like(highest)
        for k in range(n):
            total = total + bufs[k, 1:2, :] * jnp.exp(bufs[k, 0:1, :] - highest)
        return highest, total

    def added(bufs, n):
        total = bufs[0]
        for k in range(1, n):
            total = total + bufs[k]
        return total

    def to_lanes(part):
        return jnp.transpose(part)

    def to_columns(vec):
        return jnp.transpose(jnp.broadcast_to(vec, (BLK, COLS)))

    pot[...] = -exchange_rows(0, log_sum)

    def column_stats(g, carry):
        rows = pl.ds(pl.multiple_of(g * 16, 16), 16)
        tiles = [
            logits[rows, k * BLK:(k + 1) * BLK] + pot[k:k + 1, :] for k in range(SLOTS)
        ]
        highest = halving(jnp.maximum, tiles)
        tiles = [jnp.exp(tile - highest) for tile in tiles]
        for k, tile in enumerate(tiles):
            logits[rows, k * BLK:(k + 1) * BLK] = tile
        col_part[rows, :] = highest
        col_part2[rows, :] = halving(jnp.add, tiles)
        return carry

    lax.fori_loop(0, COLS // 16, column_stats, 0)
    peaks = to_lanes(col_part[...])
    sums = to_lanes(col_part2[...])
    highest = jnp.max(peaks, axis=0, keepdims=True)
    col_send0[0:1, :] = highest
    col_send0[1:2, :] = jnp.sum(sums * jnp.exp(peaks - highest), axis=0, keepdims=True)
    exchange_z(col_send0, col_buf0, 0)
    highest, total = merged(col_buf0, NZ)
    half_sq[...] = jnp.exp(col_part[...] + to_columns(BALANCE - (highest + jnp.log(total))))
    col_vec[...] = half_sq[...]

    def lanes_of(t):
        return pl.ds(pl.multiple_of(t * 4 * BLK, 4 * BLK), 4 * BLK)

    def keep_sums(p, t, values):
        sums = jnp.sum(values, axis=0, keepdims=True)
        for u in range(4):
            row_own[p, pl.ds(4 * t + u, 1), :] = sums[:, u * BLK:(u + 1) * BLK]

    def later_rows(p):
        def body(t, carry):
            keep_sums(p, t, logits[:, lanes_of(t)] * jnp.concatenate([col_vec[...]] * 4, axis=1))
            return carry

        lax.fori_loop(0, SLOTS // 4, body, 0)

    def column_sums(g, carry):
        rows = pl.ds(pl.multiple_of(g * 64, 64), 64)
        total = logits[rows, 0:BLK] * pot[0:1, :]
        for k in range(1, SLOTS):
            total = total + logits[rows, k * BLK:(k + 1) * BLK] * pot[k:k + 1, :]
        col_part[rows, :] = total * half_sq[rows, :]
        return carry

    def start_total(which):
        src = col_send.at[which - 1]
        src[...] = jnp.sum(to_lanes(col_part[...]), axis=0, keepdims=True)
        start_z(src, col_buf.at[which - 1], which)

    def finish_total(which):
        finish_z(col_buf.at[which - 1], which)
        return added(col_buf.at[which - 1], NZ)

    later_rows(1)
    pot[...] = 1.0 / exchange_rows(1, plain_sum)
    for sweep in (1, 2):
        lax.fori_loop(0, COLS // 64, column_sums, 0)
        start_total(sweep)
        col_vec[...] = half_sq[...] * to_columns((ROWS / KB) / finish_total(sweep))
        later_rows(sweep + 1)
        pot[...] = 1.0 / exchange_rows(sweep + 1, plain_sum)

    def make_transport(d):
        def body(g, carry):
            start = lax.rem(z + d + NZ, NZ) * OWN + g * 32
            rows = pl.ds(pl.multiple_of(start, 32), 32)
            col = col_vec[rows, :]
            mass = jnp.zeros((32, BLK), jnp.float32)
            for k in range(SLOTS):
                lanes = slice(k * BLK, (k + 1) * BLK)
                rounded = (logits[rows, lanes] * pot[k:k + 1, :] * col).astype(jnp.bfloat16)
                transport[rows, lanes] = rounded
                mass = mass + rounded.astype(jnp.float32)
            col_part[rows, :] = mass
            return carry

        lax.fori_loop(0, OWN // 32, body, 0)

    def weigh(d0, d1, n):
        def rows_of(d):
            return transport[pl.ds(pl.multiple_of(lax.rem(z + d + NZ, NZ) * OWN, OWN), OWN), :]

        left = jnp.concatenate([rows_of(d0), rows_of(d1)], axis=0)
        lanes = slice(n * 2 * CHUNK, (n + 1) * 2 * CHUNK)
        both = jnp.dot(left, emb[:, lanes], preferred_element_type=jnp.float32)
        partial[d0 % NZ, :, lanes] = both[:OWN]
        partial[d1 % NZ, :, lanes] = both[OWN:]

    def features(h):
        return slice(h * CHUNK, (h + 1) * CHUNK)

    def long_step(h, s):
        way = 1 - 2 * (h % 2)
        value = partial[(way * (4 - s)) % NZ, :, features(h)]
        if s:
            arrived(long_in.at[h * 4 + s - 1], long_recv_sem.at[h * 4 + s - 1])
            value = value + long_in[h * 4 + s - 1].astype(jnp.float32)
        at = h * 4 + s
        long_out[at] = value.astype(SUM_TYPE)
        send(long_out.at[at], long_in.at[at], long_send_sem.at[at], long_recv_sem.at[at], at_z(way))

    def short_step(h, s):
        way = 2 * (h % 2) - 1
        value = partial[(way * (3 - s)) % NZ, :, features(h)]
        if s:
            arrived(short_in.at[h * 3 + s - 1], short_recv_sem.at[h * 3 + s - 1])
            value = value + short_in[h * 3 + s - 1].astype(jnp.float32)
        at = h * 3 + s
        short_out[at] = value.astype(SUM_TYPE)
        send(short_out.at[at], short_in.at[at], short_send_sem.at[at], short_recv_sem.at[at], at_z(way))

    make_transport(4)
    make_transport(3)
    for n in range(CHUNKS // 2):
        weigh(4, 3, n)
        for h in (2 * n, 2 * n + 1):
            long_step(h, 0)
        short_step(2 * n + 1, 0)
    make_transport(-3)
    make_transport(2)
    for n in range(CHUNKS // 2):
        weigh(-3, 2, n)
        short_step(2 * n, 0)
    for h in range(CHUNKS):
        long_step(h, 1)
        if h % 2:
            short_step(h, 1)
    make_transport(-2)
    make_transport(1)
    for n in range(CHUNKS // 2):
        weigh(-2, 1, n)
    for n in range(CHUNKS // 2):
        short_step(2 * n, 1)
        for h in (2 * n, 2 * n + 1):
            long_step(h, 2)
        short_step(2 * n + 1, 2)
    make_transport(-1)
    make_transport(0)
    start_total(3)
    for n in range(CHUNKS // 2):
        weigh(-1, 0, n)
        short_step(2 * n, 2)
    for h in range(CHUNKS):
        long_step(h, 3)
    col_vec[...] = to_columns(finish_total(3))
    mass = col_vec[pl.ds(pl.multiple_of(z * OWN, OWN), OWN), :][:, :1]
    for h in range(CHUNKS):
        arrived(short_in.at[h * 3 + 2], short_recv_sem.at[h * 3 + 2])
        weighted = partial[0, :, features(h)] + short_in[h * 3 + 2].astype(jnp.float32)
        arrived(long_in.at[h * 4 + 3], long_recv_sem.at[h * 4 + 3])
        weighted = weighted + long_in[h * 4 + 3].astype(jnp.float32)
        grad[:, features(h)] = (mass * cent[:, features(h)] - weighted) * (KB / ROWS)

    for copy in pending:
        copy.wait_send()


def per_device(stream, sample_index, centroids, first_moment, second_moment):
    f32 = jnp.float32
    scratch = [
        pltpu.VMEM((STREAM, E), jnp.bfloat16),
        pltpu.VMEM((NR, E), jnp.bfloat16),
        pltpu.VMEM((COLS, E), jnp.bfloat16),
        pltpu.VMEM((COLS, NR), f32),
        pltpu.VMEM((COLS, NR), jnp.bfloat16),
        pltpu.VMEM((COLS, BLK), f32),
        pltpu.VMEM((COLS, BLK), f32),
        pltpu.VMEM((COLS, BLK), f32),
        pltpu.VMEM((COLS, BLK), f32),
        pltpu.VMEM((4, SLOTS, BLK), f32),
        pltpu.VMEM((4, SLOTS, BLK), f32),
        pltpu.VMEM((4, SLOTS, BLK), f32),
        pltpu.VMEM((4, PLANE, SLOTS, BLK), f32),
        pltpu.VMEM((SLOTS, BLK), f32),
        pltpu.VMEM((2, COLS), f32),
        pltpu.VMEM((3, 1, COLS), f32),
        pltpu.VMEM((NZ, 2, COLS), f32),
        pltpu.VMEM((3, NZ, 1, COLS), f32),
        pltpu.VMEM((NZ, OWN, E), f32),
        pltpu.VMEM((4 * CHUNKS, OWN, CHUNK), SUM_TYPE),
        pltpu.VMEM((3 * CHUNKS, OWN, CHUNK), SUM_TYPE),
        pltpu.VMEM((4 * CHUNKS, OWN, CHUNK), SUM_TYPE),
        pltpu.VMEM((3 * CHUNKS, OWN, CHUNK), SUM_TYPE),
        pltpu.SemaphoreType.DMA((64,)),
        pltpu.SemaphoreType.DMA((SLOTS, PARTS)),
        pltpu.SemaphoreType.DMA,
        pltpu.SemaphoreType.DMA,
        pltpu.SemaphoreType.DMA((14,)),
        pltpu.SemaphoreType.DMA((NZ, 2)),
        pltpu.SemaphoreType.DMA((4,)),
        pltpu.SemaphoreType.DMA((4,)),
        pltpu.SemaphoreType.DMA((4, PLANE - 1)),
        pltpu.SemaphoreType.DMA((4, PLANE)),
        pltpu.SemaphoreType.DMA((4, NZ - 1)),
        pltpu.SemaphoreType.DMA((4, NZ)),
        pltpu.SemaphoreType.DMA((4 * CHUNKS,)),
        pltpu.SemaphoreType.DMA((4 * CHUNKS,)),
        pltpu.SemaphoreType.DMA((3 * CHUNKS,)),
        pltpu.SemaphoreType.DMA((3 * CHUNKS,)),
        pltpu.SemaphoreType.DMA,
    ]
    gradient = pl.pallas_call(
        kernel,
        out_shape=jax.ShapeDtypeStruct((OWN, E), f32),
        in_specs=[pl.BlockSpec(memory_space=pl.ANY)] + [pl.BlockSpec(memory_space=pltpu.VMEM)] * 2,
        out_specs=pl.BlockSpec(memory_space=pltpu.VMEM),
        scratch_shapes=scratch,
        compiler_params=pltpu.CompilerParams(
            collective_id=0, has_side_effects=True, vmem_limit_bytes=56 * 1024 * 1024
        ),
        cost_estimate=pl.CostEstimate(
            flops=4 * NR * COLS * E, bytes_accessed=4 * 1024 * 1024, transcendentals=3 * NR * COLS
        ),
        name="balanced_kmeans",
    )(stream, sample_index.reshape(ND // BLK, BLK), centroids)
    new_first = beta_one * first_moment + (1.0 - beta_one) * gradient
    new_second = beta_two * second_moment + (1.0 - beta_two) * gradient * gradient
    new_centroids = centroids - step_rate * new_first / (jnp.sqrt(new_second) + epsilon)
    return (new_centroids, new_first, new_second)


def solution(mesh):
    cut = P(("cent", "dp"), None)
    return jax.shard_map(
        per_device,
        mesh=mesh,
        in_specs=(P("dp", None), P("dp"), cut, cut, cut),
        out_specs=(cut, cut, cut),
        check_vma=False,
    )
```

```python
import functools
import math

import jax
import jax.numpy as jnp
from jax import lax
from jax.experimental import pallas as pl
from jax.experimental.pallas import tpu as pltpu
from jax.sharding import PartitionSpec as P

MESH = pl.DeviceIdType.MESH

KB = 16384
ROWS = 32768
NX, NY, NZ = 4, 4, 8
E = 768
OWN = 64
COLS = OWN * NZ
ND = 1024
BLK = 128
PARTS = 2
SLOTS = NY * ND // BLK
NR = SLOTS * BLK
STREAM = 2 * ND
BALANCE = math.log(ROWS / KB)
SUM_TYPE = jnp.bfloat16
CHUNK = 384
CHUNKS = E // CHUNK
PLANE = NX * NY

beta_one = 0.9
beta_two = 0.99
step_rate = 0.05
epsilon = 1e-08


def halving(op, parts):
    while len(parts) > 1:
        parts = [op(a, b) for a, b in zip(parts[::2], parts[1::2])]
    return parts[0]


def kernel(
    stream_hbm, idx, cent, grad,
    stream,    emb, piece, logits, transport, half_sq, col_part, col_part2, col_vec,
    row_own, row_sib, row_chip, row_plane, pot,
    col_send0, col_send, col_buf0, col_buf,
    partial, long_out, short_out, long_in, short_in,
    emb_send, emb_recv, sib_send, sib_recv, z_send, z_recv,
    row_sib_send, row_sib_recv, plane_send, plane_recv, col_send_sem, col_recv_sem,
    long_send_sem, long_recv_sem, short_send_sem, short_recv_sem, load_sem,
):
    dp = lax.axis_index("dp")
    group = lax.axis_index("cent")
    y, z = dp // NZ, lax.rem(dp, NZ)
    x, core = group // 2, lax.rem(group, 2)

    def at_y(k):
        return {"dp": lax.rem(y + k + NY, NY) * NZ + z, "cent": group}

    def at_z(k):
        return {"dp": y * NZ + lax.rem(z + k + NZ, NZ), "cent": group}

    def at_x(k):
        return {"dp": dp, "cent": lax.rem(x + k + NX, NX) * 2 + core}

    def at_plane(ky, kx):
        return {"dp": lax.rem(y + ky, NY) * NZ + z, "cent": lax.rem(x + kx, NX) * 2 + core}

    sibling = {"dp": dp, "cent": x * 2 + 1 - core}

    barrier = pltpu.get_barrier_semaphore()
    for device in (sibling, at_x(1), at_x(-1), at_y(1), at_y(-1), at_z(1), at_z(-1)):
        pl.semaphore_signal(barrier, inc=1, device_id=device, device_id_type=MESH)
    load = pltpu.make_async_copy(stream_hbm, stream, load_sem)
    load.start()

    pending = []

    def send(src, dst, send_sem, recv_sem, device):
        copy = pltpu.make_async_remote_copy(
            src_ref=src, dst_ref=dst, send_sem=send_sem, recv_sem=recv_sem,
            device_id=device, device_id_type=MESH,
        )
        copy.start()
        pending.append(copy)

    def arrived(dst, recv_sem):
        pltpu.make_async_remote_copy(
            src_ref=dst, dst_ref=dst, send_sem=recv_sem, recv_sem=recv_sem,
            device_id=sibling, device_id_type=MESH,
        ).wait_recv()

    def slot_of(k, c, j):
        return lax.rem(y + k + NY, NY) * 8 + c * 4 + lax.rem(x + j, 4)

    def emb_at(slot, count=1):
        return emb.at[pl.ds(pl.multiple_of(slot * BLK, BLK), count * BLK), :]

    sends = [0]

    def send_block(slot, device):
        send(emb_at(slot), emb_at(slot), emb_send.at[sends[0]], emb_recv.at[slot, 0], device)
        sends[0] += 1

    def wait_block(slot):
        arrived(emb_at(slot), emb_recv.at[slot, 0])

    def part_at(slot, h):
        return emb.at[pl.ds(pl.multiple_of(slot * BLK + h * (BLK // PARTS), BLK // PARTS), BLK // PARTS), :]

    def send_part(slot, h, device):
        send(part_at(slot, h), part_at(slot, h), emb_send.at[sends[0]], emb_recv.at[slot, h], device)
        sends[0] += 1

    def piece_at(k, h):
        owner = lax.rem(z + k + NZ, NZ)
        return piece.at[pl.ds(pl.multiple_of(owner * OWN + h * (OWN // 2), OWN // 2), OWN // 2), :]

    z_sends = [0]

    def send_piece(k, h, toward):
        owner = lax.rem(z + k + NZ, NZ)
        send(piece_at(k, h), piece_at(k, h), z_send.at[z_sends[0]], z_recv.at[owner, h], at_z(toward))
        z_sends[0] += 1

    def on_pieces(k, h, forward=True):
        for d in (-k, k):
            arrived(piece_at(d, h), z_recv.at[lax.rem(z + d + NZ, NZ), h])
            if forward or (d == -3):
                send_piece(d, h, 1 if d < 0 else -1)

    def gather(j):
        quarter = lax.rem(x + j, 4)
        picked = idx[pl.ds(core * 4 + quarter, 1), :].astype(jnp.float32)
        column = jnp.broadcast_to(picked, (BLK, BLK)).T[:, :1]
        place = lax.broadcasted_iota(jnp.int32, (BLK, STREAM), 1).astype(jnp.float32)
        one_hot = jnp.where(place == column, 1.0, 0.0).astype(jnp.bfloat16)
        rows = jnp.dot(one_hot, stream[...], preferred_element_type=jnp.float32)
        slot = slot_of(0, core, j)
        emb[pl.ds(pl.multiple_of(slot * BLK, BLK), BLK), :] = rows.astype(jnp.bfloat16)
        return slot

    piece[pl.ds(pl.multiple_of(z * OWN, OWN), OWN), :] = cent[...].astype(jnp.bfloat16)
    load.wait()
    first = gather(0)
    pl.semaphore_wait(barrier, 7)
    for h in range(PARTS):
        send_part(first, h, at_y(1))
        send_part(first, h, at_y(-1))
    for h in (0, 1):
        send_piece(0, h, 1)
        send_piece(0, h, -1)
    second = gather(2)
    gather(1)
    gather(3)
    own_first = y * 8 + core * 4
    send(emb_at(own_first, 4), emb_at(own_first, 4), sib_send, sib_recv, sibling)

    def on_part(k, j, h, forward=False, spread=False):
        slot = slot_of(k, core, j)
        arrived(part_at(slot, h), emb_recv.at[slot, h])
        if forward:
            send_part(slot, h, at_y(1))
        if spread:
            send_part(slot, h, at_x(1))
            send_part(slot, h, at_x(-1))
        if h == PARTS - 1:
            send_block(slot, sibling)

    def on_block(k, j, forward=False):
        slot = slot_of(k, core, j)
        wait_block(slot)
        if forward:
            send_block(slot, at_y(-1))
        send_block(slot, sibling)

    def score(blocks):
        starts = [pl.multiple_of(slot * BLK, BLK) for slot in blocks]
        rows = jnp.concatenate([emb[pl.ds(start, BLK), :] for start in starts], axis=0)
        product = lax.dot_general(
            piece[...], rows, (((1,), (1,)), ((), ())), preferred_element_type=jnp.float32
        )
        less = half_sq[...]
        for k, start in enumerate(starts):
            lanes = pl.ds(start, BLK)
            values = product[:, k * BLK:(k + 1) * BLK] - less
            logits[:, lanes] = values
            highest = jnp.max(values, axis=0, keepdims=True)
            total = jnp.sum(jnp.exp(values - highest), axis=0, keepdims=True)
            row_own[0, pl.ds(blocks[k], 1), :] = highest + jnp.log(total)

    def score_from(offsets, c):
        blocks = [slot_of(k, c, j) for k, j in offsets]
        if offsets[0][0] and c is not core:
            for slot in blocks:
                wait_block(slot)
        score(blocks)

    own = [(0, 0), (0, 1), (0, 2), (0, 3)]
    early = [(-1, 0), (1, 0), (2, 0), (1, 2)]
    middle = [(-1, 1), (-1, 3), (1, 1), (1, 3)]
    late = [(-1, 2), (2, 2), (2, 1), (2, 3)]
    other = 1 - core

    on_pieces(1, 0)
    for h in range(PARTS):
        on_part(-1, 0, h, forward=True, spread=True)
        on_part(1, 0, h, spread=True)
        if h == PARTS // 2 - 1:
            on_pieces(1, 1)
            send_block(second, at_y(-1))
    send_block(second, at_y(1))
    on_pieces(2, 0)
    on_pieces(2, 1)
    for h in range(PARTS):
        on_part(2, 0, h, spread=True)
        if h == PARTS // 2 - 1:
            on_pieces(3, 0, False)
    on_pieces(3, 1, False)
    on_block(1, 2, forward=True)
    for h in range(PARTS):
        on_part(-1, 1, h)
        on_part(-1, 3, h)
    for h in (0, 1):
        arrived(piece_at(-4, h), z_recv.at[lax.rem(z + 4, NZ), h])
    whole = piece[...].astype(jnp.float32)
    half_sq[...] = jnp.broadcast_to(
        0.5 * jnp.sum(whole * whole, axis=1, keepdims=True), (COLS, BLK)
    )
    score_from(own, core)
    score_from(early, core)
    arrived(emb_at(y * 8 + other * 4, 4), sib_recv)
    score_from(own, other)
    for h in range(PARTS):
        on_part(1, 1, h)
        on_part(1, 3, h)
    on_block(-1, 2)
    score_from(early, other)
    score_from(middle, core)
    on_block(2, 2)
    for h in range(PARTS):
        on_part(2, 1, h)
        on_part(2, 3, h)
    score_from(middle, other)
    score_from(late, core)
    score_from(late, other)

    plane_peers = [(ky, kx) for ky in (2, 1, 3, 0) for kx in (2, 1, 3, 0) if ky or kx]

    def exchange_rows(p, combine):
        send(row_own.at[p], row_sib.at[p], row_sib_send.at[p], row_sib_recv.at[p], sibling)
        arrived(row_sib.at[p], row_sib_recv.at[p])
        chip = combine([row_own[p], row_sib[p]])
        row_chip[p] = chip
        me = y * NX + x
        for at, (ky, kx) in enumerate(plane_peers):
            send(row_chip.at[p], row_plane.at[p, me], plane_send.at[p, at], plane_recv.at[p, me], at_plane(ky, kx))
        row_plane[p, me] = chip
        for ky, kx in reversed(plane_peers):
            peer = lax.rem(y + ky, NY) * NX + lax.rem(x + kx, NX)
            arrived(row_plane.at[p, peer], plane_recv.at[p, peer])
        return combine([row_plane[p, k] for k in range(PLANE)])

    def log_sum(parts):
        highest = functools.reduce(jnp.maximum, parts)
        total = functools.reduce(jnp.add, [jnp.exp(part - highest) for part in parts])
        return highest + jnp.log(total)

    def plain_sum(parts):
        return functools.reduce(jnp.add, parts)

    def start_z(src, bufs, which):
        for k in range(1, NZ):
            send(
                src, bufs.at[z],
                col_send_sem.at[which, k - 1], col_recv_sem.at[which, z], at_z(k),
            )
        bufs[z] = src[...]

    def finish_z(bufs, which):
        for k in range(1, NZ):
            other = lax.rem(z + k, NZ)
            arrived(bufs.at[other], col_recv_sem.at[which, other])

    def exchange_z(src, bufs, which):
        start_z(src, bufs, which)
        finish_z(bufs, which)

    def merged(bufs, n):
        highest = bufs[0, 0:1, :]
        for k in range(1, n):
            highest = jnp.maximum(highest, bufs[k, 0:1, :])
        total = jnp.zeros_like(highest)
        for k in range(n):
            total = total + bufs[k, 1:2, :] * jnp.exp(bufs[k, 0:1, :] - highest)
        return highest, total

    def added(bufs, n):
        total = bufs[0]
        for k in range(1, n):
            total = total + bufs[k]
        return total

    def to_lanes(part):
        return jnp.transpose(part)

    def to_columns(vec):
        return jnp.transpose(jnp.broadcast_to(vec, (BLK, COLS)))

    pot[...] = -exchange_rows(0, log_sum)

    def column_stats(g, carry):
        rows = pl.ds(pl.multiple_of(g * 16, 16), 16)
        tiles = [
            logits[rows, k * BLK:(k + 1) * BLK] + pot[k:k + 1, :] for k in range(SLOTS)
        ]
        highest = halving(jnp.maximum, tiles)
        tiles = [jnp.exp(tile - highest) for tile in tiles]
        for k, tile in enumerate(tiles):
            logits[rows, k * BLK:(k + 1) * BLK] = tile
        col_part[rows, :] = highest
        col_part2[rows, :] = halving(jnp.add, tiles)
        return carry

    lax.fori_loop(0, COLS // 16, column_stats, 0)
    peaks = to_lanes(col_part[...])
    sums = to_lanes(col_part2[...])
    highest = jnp.max(peaks, axis=0, keepdims=True)
    col_send0[0:1, :] = highest
    col_send0[1:2, :] = jnp.sum(sums * jnp.exp(peaks - highest), axis=0, keepdims=True)
    exchange_z(col_send0, col_buf0, 0)
    highest, total = merged(col_buf0, NZ)
    half_sq[...] = jnp.exp(col_part[...] + to_columns(BALANCE - (highest + jnp.log(total))))
    col_vec[...] = half_sq[...]

    def lanes_of(t):
        return pl.ds(pl.multiple_of(t * 8 * BLK, 8 * BLK), 8 * BLK)

    def keep_sums(p, t, values):
        sums = jnp.sum(values, axis=0, keepdims=True)
        for u in range(8):
            row_own[p, pl.ds(8 * t + u, 1), :] = sums[:, u * BLK:(u + 1) * BLK]

    def later_rows(p):
        def body(t, carry):
            keep_sums(p, t, logits[:, lanes_of(t)] * jnp.concatenate([col_vec[...]] * 8, axis=1))
            return carry

        lax.fori_loop(0, SLOTS // 8, body, 0)

    def column_sums(g, carry):
        rows = pl.ds(pl.multiple_of(g * 128, 128), 128)
        total = logits[rows, 0:BLK] * pot[0:1, :]
        for k in range(1, SLOTS):
            total = total + logits[rows, k * BLK:(k + 1) * BLK] * pot[k:k + 1, :]
        col_part[rows, :] = total * half_sq[rows, :]
        return carry

    def start_total(which):
        src = col_send.at[which - 1]
        src[...] = jnp.sum(to_lanes(col_part[...]), axis=0, keepdims=True)
        start_z(src, col_buf.at[which - 1], which)

    def finish_total(which):
        finish_z(col_buf.at[which - 1], which)
        return added(col_buf.at[which - 1], NZ)

    later_rows(1)
    pot[...] = 1.0 / exchange_rows(1, plain_sum)
    for sweep in (1, 2):
        lax.fori_loop(0, COLS // 128, column_sums, 0)
        start_total(sweep)
        col_vec[...] = half_sq[...] * to_columns((ROWS / KB) / finish_total(sweep))
        later_rows(sweep + 1)
        pot[...] = 1.0 / exchange_rows(sweep + 1, plain_sum)

    def make_transport(d):
        def body(g, carry):
            start = lax.rem(z + d + NZ, NZ) * OWN + g * 32
            rows = pl.ds(pl.multiple_of(start, 32), 32)
            col = col_vec[rows, :]
            mass = jnp.zeros((32, BLK), jnp.float32)
            for k in range(SLOTS):
                lanes = slice(k * BLK, (k + 1) * BLK)
                rounded = (logits[rows, lanes] * pot[k:k + 1, :] * col).astype(jnp.bfloat16)
                transport[rows, lanes] = rounded
                mass = mass + rounded.astype(jnp.float32)
            col_part[rows, :] = mass
            return carry

        lax.fori_loop(0, OWN // 32, body, 0)

    def weigh(d0, d1, n):
        def rows_of(d):
            return transport[pl.ds(pl.multiple_of(lax.rem(z + d + NZ, NZ) * OWN, OWN), OWN), :]

        left = jnp.concatenate([rows_of(d0), rows_of(d1)], axis=0)
        lanes = slice(n * 2 * CHUNK, (n + 1) * 2 * CHUNK)
        both = jnp.dot(left, emb[:, lanes], preferred_element_type=jnp.float32)
        partial[d0 % NZ, :, lanes] = both[:OWN]
        partial[d1 % NZ, :, lanes] = both[OWN:]

    def features(h):
        return slice(h * CHUNK, (h + 1) * CHUNK)

    def long_step(h, s):
        way = 1 - 2 * (h % 2)
        value = partial[(way * (4 - s)) % NZ, :, features(h)]
        if s:
            arrived(long_in.at[h * 4 + s - 1], long_recv_sem.at[h * 4 + s - 1])
            value = value + long_in[h * 4 + s - 1].astype(jnp.float32)
        at = h * 4 + s
        long_out[at] = value.astype(SUM_TYPE)
        send(long_out.at[at], long_in.at[at], long_send_sem.at[at], long_recv_sem.at[at], at_z(way))

    def short_step(h, s):
        way = 2 * (h % 2) - 1
        value = partial[(way * (3 - s)) % NZ, :, features(h)]
        if s:
            arrived(short_in.at[h * 3 + s - 1], short_recv_sem.at[h * 3 + s - 1])
            value = value + short_in[h * 3 + s - 1].astype(jnp.float32)
        at = h * 3 + s
        short_out[at] = value.astype(SUM_TYPE)
        send(short_out.at[at], short_in.at[at], short_send_sem.at[at], short_recv_sem.at[at], at_z(way))

    make_transport(4)
    make_transport(3)
    for n in range(CHUNKS // 2):
        weigh(4, 3, n)
        for h in (2 * n, 2 * n + 1):
            long_step(h, 0)
        short_step(2 * n + 1, 0)
    make_transport(-3)
    make_transport(2)
    for n in range(CHUNKS // 2):
        weigh(-3, 2, n)
        short_step(2 * n, 0)
    for h in range(CHUNKS):
        long_step(h, 1)
        if h % 2:
            short_step(h, 1)
    make_transport(-2)
    make_transport(1)
    for n in range(CHUNKS // 2):
        weigh(-2, 1, n)
    for n in range(CHUNKS // 2):
        short_step(2 * n, 1)
        for h in (2 * n, 2 * n + 1):
            long_step(h, 2)
        short_step(2 * n + 1, 2)
    make_transport(-1)
    make_transport(0)
    start_total(3)
    for n in range(CHUNKS // 2):
        weigh(-1, 0, n)
        short_step(2 * n, 2)
    for h in range(CHUNKS):
        long_step(h, 3)
    col_vec[...] = to_columns(finish_total(3))
    mass = col_vec[pl.ds(pl.multiple_of(z * OWN, OWN), OWN), :][:, :1]
    for h in range(CHUNKS):
        arrived(short_in.at[h * 3 + 2], short_recv_sem.at[h * 3 + 2])
        weighted = partial[0, :, features(h)] + short_in[h * 3 + 2].astype(jnp.float32)
        arrived(long_in.at[h * 4 + 3], long_recv_sem.at[h * 4 + 3])
        weighted = weighted + long_in[h * 4 + 3].astype(jnp.float32)
        grad[:, features(h)] = (mass * cent[:, features(h)] - weighted) * (KB / ROWS)

    for copy in pending:
        copy.wait_send()


def per_device(stream, sample_index, centroids, first_moment, second_moment):
    f32 = jnp.float32
    scratch = [
        pltpu.VMEM((STREAM, E), jnp.bfloat16),
        pltpu.VMEM((NR, E), jnp.bfloat16),
        pltpu.VMEM((COLS, E), jnp.bfloat16),
        pltpu.VMEM((COLS, NR), f32),
        pltpu.VMEM((COLS, NR), jnp.bfloat16),
        pltpu.VMEM((COLS, BLK), f32),
        pltpu.VMEM((COLS, BLK), f32),
        pltpu.VMEM((COLS, BLK), f32),
        pltpu.VMEM((COLS, BLK), f32),
        pltpu.VMEM((4, SLOTS, BLK), f32),
        pltpu.VMEM((4, SLOTS, BLK), f32),
        pltpu.VMEM((4, SLOTS, BLK), f32),
        pltpu.VMEM((4, PLANE, SLOTS, BLK), f32),
        pltpu.VMEM((SLOTS, BLK), f32),
        pltpu.VMEM((2, COLS), f32),
        pltpu.VMEM((3, 1, COLS), f32),
        pltpu.VMEM((NZ, 2, COLS), f32),
        pltpu.VMEM((3, NZ, 1, COLS), f32),
        pltpu.VMEM((NZ, OWN, E), f32),
        pltpu.VMEM((4 * CHUNKS, OWN, CHUNK), SUM_TYPE),
        pltpu.VMEM((3 * CHUNKS, OWN, CHUNK), SUM_TYPE),
        pltpu.VMEM((4 * CHUNKS, OWN, CHUNK), SUM_TYPE),
        pltpu.VMEM((3 * CHUNKS, OWN, CHUNK), SUM_TYPE),
        pltpu.SemaphoreType.DMA((64,)),
        pltpu.SemaphoreType.DMA((SLOTS, PARTS)),
        pltpu.SemaphoreType.DMA,
        pltpu.SemaphoreType.DMA,
        pltpu.SemaphoreType.DMA((14,)),
        pltpu.SemaphoreType.DMA((NZ, 2)),
        pltpu.SemaphoreType.DMA((4,)),
        pltpu.SemaphoreType.DMA((4,)),
        pltpu.SemaphoreType.DMA((4, PLANE - 1)),
        pltpu.SemaphoreType.DMA((4, PLANE)),
        pltpu.SemaphoreType.DMA((4, NZ - 1)),
        pltpu.SemaphoreType.DMA((4, NZ)),
        pltpu.SemaphoreType.DMA((4 * CHUNKS,)),
        pltpu.SemaphoreType.DMA((4 * CHUNKS,)),
        pltpu.SemaphoreType.DMA((3 * CHUNKS,)),
        pltpu.SemaphoreType.DMA((3 * CHUNKS,)),
        pltpu.SemaphoreType.DMA,
    ]
    gradient = pl.pallas_call(
        kernel,
        out_shape=jax.ShapeDtypeStruct((OWN, E), f32),
        in_specs=[pl.BlockSpec(memory_space=pl.ANY)] + [pl.BlockSpec(memory_space=pltpu.VMEM)] * 2,
        out_specs=pl.BlockSpec(memory_space=pltpu.VMEM),
        scratch_shapes=scratch,
        compiler_params=pltpu.CompilerParams(
            collective_id=0, has_side_effects=True, vmem_limit_bytes=56 * 1024 * 1024
        ),
        cost_estimate=pl.CostEstimate(
            flops=4 * NR * COLS * E, bytes_accessed=4 * 1024 * 1024, transcendentals=3 * NR * COLS
        ),
        name="balanced_kmeans",
    )(stream, sample_index.reshape(ND // BLK, BLK), centroids)
    new_first = beta_one * first_moment + (1.0 - beta_one) * gradient
    new_second = beta_two * second_moment + (1.0 - beta_two) * gradient * gradient
    new_centroids = centroids - step_rate * new_first / (jnp.sqrt(new_second) + epsilon)
    return (new_centroids, new_first, new_second)


def solution(mesh):
    cut = P(("cent", "dp"), None)
    return jax.shard_map(
        per_device,
        mesh=mesh,
        in_specs=(P("dp", None), P("dp"), cut, cut, cut),
        out_specs=(cut, cut, cut),
        check_vma=False,
    )
```

```python
import functools
import math

import jax
import jax.numpy as jnp
from jax import lax
from jax.experimental import pallas as pl
from jax.experimental.pallas import tpu as pltpu
from jax.sharding import PartitionSpec as P

MESH = pl.DeviceIdType.MESH

KB = 16384
ROWS = 32768
NX, NY, NZ = 4, 4, 8
E = 768
OWN = 64
COLS = OWN * NZ
ND = 1024
BLK = 128
PARTS = 2
SLOTS = NY * ND // BLK
NR = SLOTS * BLK
STREAM = 2 * ND
BALANCE = math.log(ROWS / KB)
SUM_TYPE = jnp.bfloat16
CHUNK = 384
CHUNKS = E // CHUNK
PLANE = NX * NY

beta_one = 0.9
beta_two = 0.99
step_rate = 0.05
epsilon = 1e-08


def halving(op, parts):
    while len(parts) > 1:
        parts = [op(a, b) for a, b in zip(parts[::2], parts[1::2])]
    return parts[0]


def kernel(
    stream_hbm, idx, cent, grad,
    stream,    emb, piece, logits, transport, half_sq, col_part, col_part2, col_vec,
    row_own, row_sib, row_chip, row_plane, pot,
    col_send0, col_send, col_buf0, col_buf,
    partial, long_out, short_out, long_in, short_in,
    emb_send, emb_recv, sib_send, sib_recv, z_send, z_recv,
    row_sib_send, row_sib_recv, plane_send, plane_recv, col_send_sem, col_recv_sem,
    long_send_sem, long_recv_sem, short_send_sem, short_recv_sem, load_sem,
):
    dp = lax.axis_index("dp")
    group = lax.axis_index("cent")
    y, z = dp // NZ, lax.rem(dp, NZ)
    x, core = group // 2, lax.rem(group, 2)

    def at_y(k):
        return {"dp": lax.rem(y + k + NY, NY) * NZ + z, "cent": group}

    def at_z(k):
        return {"dp": y * NZ + lax.rem(z + k + NZ, NZ), "cent": group}

    def at_x(k):
        return {"dp": dp, "cent": lax.rem(x + k + NX, NX) * 2 + core}

    def at_plane(ky, kx):
        return {"dp": lax.rem(y + ky, NY) * NZ + z, "cent": lax.rem(x + kx, NX) * 2 + core}

    sibling = {"dp": dp, "cent": x * 2 + 1 - core}

    barrier = pltpu.get_barrier_semaphore()
    for device in (sibling, at_x(1), at_x(-1), at_y(1), at_y(-1), at_z(1), at_z(-1)):
        pl.semaphore_signal(barrier, inc=1, device_id=device, device_id_type=MESH)
    load = pltpu.make_async_copy(stream_hbm, stream, load_sem)
    load.start()

    pending = []

    def send(src, dst, send_sem, recv_sem, device):
        copy = pltpu.make_async_remote_copy(
            src_ref=src, dst_ref=dst, send_sem=send_sem, recv_sem=recv_sem,
            device_id=device, device_id_type=MESH,
        )
        copy.start()
        pending.append(copy)

    def arrived(dst, recv_sem):
        pltpu.make_async_remote_copy(
            src_ref=dst, dst_ref=dst, send_sem=recv_sem, recv_sem=recv_sem,
            device_id=sibling, device_id_type=MESH,
        ).wait_recv()

    def slot_of(k, c, j):
        return lax.rem(y + k + NY, NY) * 8 + c * 4 + lax.rem(x + j, 4)

    def emb_at(slot, count=1):
        return emb.at[pl.ds(pl.multiple_of(slot * BLK, BLK), count * BLK), :]

    sends = [0]

    def send_block(slot, device):
        send(emb_at(slot), emb_at(slot), emb_send.at[sends[0]], emb_recv.at[slot, 0], device)
        sends[0] += 1

    def wait_block(slot):
        arrived(emb_at(slot), emb_recv.at[slot, 0])

    def part_at(slot, h):
        return emb.at[pl.ds(pl.multiple_of(slot * BLK + h * (BLK // PARTS), BLK // PARTS), BLK // PARTS), :]

    def send_part(slot, h, device):
        send(part_at(slot, h), part_at(slot, h), emb_send.at[sends[0]], emb_recv.at[slot, h], device)
        sends[0] += 1

    def piece_at(k, h):
        owner = lax.rem(z + k + NZ, NZ)
        return piece.at[pl.ds(pl.multiple_of(owner * OWN + h * (OWN // 2), OWN // 2), OWN // 2), :]

    z_sends = [0]

    def send_piece(k, h, toward):
        owner = lax.rem(z + k + NZ, NZ)
        send(piece_at(k, h), piece_at(k, h), z_send.at[z_sends[0]], z_recv.at[owner, h], at_z(toward))
        z_sends[0] += 1

    def on_pieces(k, h, forward=True):
        for d in (-k, k):
            arrived(piece_at(d, h), z_recv.at[lax.rem(z + d + NZ, NZ), h])
            if forward or (d == -3):
                send_piece(d, h, 1 if d < 0 else -1)

    def gather(j):
        quarter = lax.rem(x + j, 4)
        picked = idx[pl.ds(core * 4 + quarter, 1), :].astype(jnp.float32)
        column = jnp.broadcast_to(picked, (BLK, BLK)).T[:, :1]
        place = lax.broadcasted_iota(jnp.int32, (BLK, STREAM), 1).astype(jnp.float32)
        one_hot = jnp.where(place == column, 1.0, 0.0).astype(jnp.bfloat16)
        rows = jnp.dot(one_hot, stream[...], preferred_element_type=jnp.float32)
        slot = slot_of(0, core, j)
        emb[pl.ds(pl.multiple_of(slot * BLK, BLK), BLK), :] = rows.astype(jnp.bfloat16)
        return slot

    piece[pl.ds(pl.multiple_of(z * OWN, OWN), OWN), :] = cent[...].astype(jnp.bfloat16)
    load.wait()
    first = gather(0)
    pl.semaphore_wait(barrier, 7)
    for h in range(PARTS):
        send_part(first, h, at_y(1))
        send_part(first, h, at_y(-1))
    for h in (0, 1):
        send_piece(0, h, 1)
        send_piece(0, h, -1)
    second = gather(2)
    gather(1)
    gather(3)
    own_first = y * 8 + core * 4
    send(emb_at(own_first, 4), emb_at(own_first, 4), sib_send, sib_recv, sibling)

    def on_part(k, j, h, forward=False, spread=False):
        slot = slot_of(k, core, j)
        arrived(part_at(slot, h), emb_recv.at[slot, h])
        if forward:
            send_part(slot, h, at_y(1))
        if spread:
            send_part(slot, h, at_x(1))
            send_part(slot, h, at_x(-1))
        if h == PARTS - 1:
            send_block(slot, sibling)

    def on_block(k, j, forward=False):
        slot = slot_of(k, core, j)
        wait_block(slot)
        if forward:
            send_block(slot, at_y(-1))
        send_block(slot, sibling)

    def score(blocks):
        starts = [pl.multiple_of(slot * BLK, BLK) for slot in blocks]
        rows = jnp.concatenate([emb[pl.ds(start, BLK), :] for start in starts], axis=0)
        product = lax.dot_general(
            piece[...], rows, (((1,), (1,)), ((), ())), preferred_element_type=jnp.float32
        )
        less = half_sq[...]
        for k, start in enumerate(starts):
            lanes = pl.ds(start, BLK)
            values = product[:, k * BLK:(k + 1) * BLK] - less
            logits[:, lanes] = values
            highest = jnp.max(values, axis=0, keepdims=True)
            total = jnp.sum(jnp.exp(values - highest), axis=0, keepdims=True)
            row_own[0, pl.ds(blocks[k], 1), :] = highest + jnp.log(total)

    def score_from(offsets, c):
        blocks = [slot_of(k, c, j) for k, j in offsets]
        if offsets[0][0] and c is not core:
            for slot in blocks:
                wait_block(slot)
        score(blocks)

    own = [(0, 0), (0, 1), (0, 2), (0, 3)]
    early = [(-1, 0), (1, 0), (2, 0), (1, 2)]
    middle = [(-1, 1), (-1, 3), (1, 1), (1, 3)]
    late = [(-1, 2), (2, 2), (2, 1), (2, 3)]
    other = 1 - core

    on_pieces(1, 0)
    for h in range(PARTS):
        on_part(-1, 0, h, forward=True, spread=True)
        on_part(1, 0, h, spread=True)
        if h == PARTS // 2 - 1:
            on_pieces(1, 1)
            send_block(second, at_y(-1))
    send_block(second, at_y(1))
    on_pieces(2, 0)
    on_pieces(2, 1)
    for h in range(PARTS):
        on_part(2, 0, h, spread=True)
        if h == PARTS // 2 - 1:
            on_pieces(3, 0, False)
    on_pieces(3, 1, False)
    on_block(1, 2, forward=True)
    for h in range(PARTS):
        on_part(-1, 1, h)
        on_part(-1, 3, h)
    for h in (0, 1):
        arrived(piece_at(-4, h), z_recv.at[lax.rem(z + 4, NZ), h])
    whole = piece[...].astype(jnp.float32)
    half_sq[...] = jnp.broadcast_to(
        0.5 * jnp.sum(whole * whole, axis=1, keepdims=True), (COLS, BLK)
    )
    score_from(own, core)
    score_from(early, core)
    arrived(emb_at(y * 8 + other * 4, 4), sib_recv)
    score_from(own, other)
    for h in range(PARTS):
        on_part(1, 1, h)
        on_part(1, 3, h)
    on_block(-1, 2)
    score_from(early, other)
    score_from(middle, core)
    on_block(2, 2)
    for h in range(PARTS):
        on_part(2, 1, h)
        on_part(2, 3, h)
    score_from(middle, other)
    score_from(late, core)
    score_from(late, other)

    plane_peers = [(ky, kx) for ky in (2, 1, 3, 0) for kx in (2, 1, 3, 0) if ky or kx]

    def exchange_rows(p, combine):
        send(row_own.at[p], row_sib.at[p], row_sib_send.at[p], row_sib_recv.at[p], sibling)
        arrived(row_sib.at[p], row_sib_recv.at[p])
        chip = combine([row_own[p], row_sib[p]])
        row_chip[p] = chip
        me = y * NX + x
        for at, (ky, kx) in enumerate(plane_peers):
            send(row_chip.at[p], row_plane.at[p, me], plane_send.at[p, at], plane_recv.at[p, me], at_plane(ky, kx))
        row_plane[p, me] = chip
        for ky, kx in reversed(plane_peers):
            peer = lax.rem(y + ky, NY) * NX + lax.rem(x + kx, NX)
            arrived(row_plane.at[p, peer], plane_recv.at[p, peer])
        return combine([row_plane[p, k] for k in range(PLANE)])

    def log_sum(parts):
        highest = functools.reduce(jnp.maximum, parts)
        total = functools.reduce(jnp.add, [jnp.exp(part - highest) for part in parts])
        return highest + jnp.log(total)

    def plain_sum(parts):
        return functools.reduce(jnp.add, parts)

    def start_z(src, bufs, which):
        for k in range(1, NZ):
            send(
                src, bufs.at[z],
                col_send_sem.at[which, k - 1], col_recv_sem.at[which, z], at_z(k),
            )
        bufs[z] = src[...]

    def finish_z(bufs, which):
        for k in range(1, NZ):
            other = lax.rem(z + k, NZ)
            arrived(bufs.at[other], col_recv_sem.at[which, other])

    def exchange_z(src, bufs, which):
        start_z(src, bufs, which)
        finish_z(bufs, which)

    def merged(bufs, n):
        highest = bufs[0, 0:1, :]
        for k in range(1, n):
            highest = jnp.maximum(highest, bufs[k, 0:1, :])
        total = jnp.zeros_like(highest)
        for k in range(n):
            total = total + bufs[k, 1:2, :] * jnp.exp(bufs[k, 0:1, :] - highest)
        return highest, total

    def added(bufs, n):
        total = bufs[0]
        for k in range(1, n):
            total = total + bufs[k]
        return total

    def to_lanes(part):
        return jnp.transpose(part)

    def to_columns(vec):
        return jnp.transpose(jnp.broadcast_to(vec, (BLK, COLS)))

    pot[...] = -exchange_rows(0, log_sum)

    def column_stats(g, carry):
        rows = pl.ds(pl.multiple_of(g * 32, 32), 32)
        tiles = [
            logits[rows, k * BLK:(k + 1) * BLK] + pot[k:k + 1, :] for k in range(SLOTS)
        ]
        highest = halving(jnp.maximum, tiles)
        tiles = [jnp.exp(tile - highest) for tile in tiles]
        for k, tile in enumerate(tiles):
            logits[rows, k * BLK:(k + 1) * BLK] = tile
        col_part[rows, :] = highest
        col_part2[rows, :] = halving(jnp.add, tiles)
        return carry

    lax.fori_loop(0, COLS // 32, column_stats, 0)
    peaks = to_lanes(col_part[...])
    sums = to_lanes(col_part2[...])
    highest = jnp.max(peaks, axis=0, keepdims=True)
    col_send0[0:1, :] = highest
    col_send0[1:2, :] = jnp.sum(sums * jnp.exp(peaks - highest), axis=0, keepdims=True)
    exchange_z(col_send0, col_buf0, 0)
    highest, total = merged(col_buf0, NZ)
    half_sq[...] = jnp.exp(col_part[...] + to_columns(BALANCE - (highest + jnp.log(total))))
    col_vec[...] = half_sq[...]

    def lanes_of(t):
        return pl.ds(pl.multiple_of(t * 8 * BLK, 8 * BLK), 8 * BLK)

    def keep_sums(p, t, values):
        sums = jnp.sum(values, axis=0, keepdims=True)
        for u in range(8):
            row_own[p, pl.ds(8 * t + u, 1), :] = sums[:, u * BLK:(u + 1) * BLK]

    def later_rows(p):
        def body(t, carry):
            keep_sums(p, t, logits[:, lanes_of(t)] * jnp.concatenate([col_vec[...]] * 8, axis=1))
            return carry

        lax.fori_loop(0, SLOTS // 8, body, 0)

    def column_sums(g, carry):
        rows = pl.ds(pl.multiple_of(g * 256, 256), 256)
        total = logits[rows, 0:BLK] * pot[0:1, :]
        for k in range(1, SLOTS):
            total = total + logits[rows, k * BLK:(k + 1) * BLK] * pot[k:k + 1, :]
        col_part[rows, :] = total * half_sq[rows, :]
        return carry

    def start_total(which):
        src = col_send.at[which - 1]
        src[...] = jnp.sum(to_lanes(col_part[...]), axis=0, keepdims=True)
        start_z(src, col_buf.at[which - 1], which)

    def finish_total(which):
        finish_z(col_buf.at[which - 1], which)
        return added(col_buf.at[which - 1], NZ)

    later_rows(1)
    pot[...] = 1.0 / exchange_rows(1, plain_sum)
    for sweep in (1, 2):
        lax.fori_loop(0, COLS // 256, column_sums, 0)
        start_total(sweep)
        col_vec[...] = half_sq[...] * to_columns((ROWS / KB) / finish_total(sweep))
        later_rows(sweep + 1)
        pot[...] = 1.0 / exchange_rows(sweep + 1, plain_sum)

    def make_transport(d):
        def body(g, carry):
            start = lax.rem(z + d + NZ, NZ) * OWN + g * 32
            rows = pl.ds(pl.multiple_of(start, 32), 32)
            col = col_vec[rows, :]
            mass = jnp.zeros((32, BLK), jnp.float32)
            for k in range(SLOTS):
                lanes = slice(k * BLK, (k + 1) * BLK)
                rounded = (logits[rows, lanes] * pot[k:k + 1, :] * col).astype(jnp.bfloat16)
                transport[rows, lanes] = rounded
                mass = mass + rounded.astype(jnp.float32)
            col_part[rows, :] = mass
            return carry

        lax.fori_loop(0, OWN // 32, body, 0)

    def weigh(d0, d1, n):
        def rows_of(d):
            return transport[pl.ds(pl.multiple_of(lax.rem(z + d + NZ, NZ) * OWN, OWN), OWN), :]

        left = jnp.concatenate([rows_of(d0), rows_of(d1)], axis=0)
        lanes = slice(n * 2 * CHUNK, (n + 1) * 2 * CHUNK)
        both = jnp.dot(left, emb[:, lanes], preferred_element_type=jnp.float32)
        partial[d0 % NZ, :, lanes] = both[:OWN]
        partial[d1 % NZ, :, lanes] = both[OWN:]

    def features(h):
        return slice(h * CHUNK, (h + 1) * CHUNK)

    def long_step(h, s):
        way = 1 - 2 * (h % 2)
        value = partial[(way * (4 - s)) % NZ, :, features(h)]
        if s:
            arrived(long_in.at[h * 4 + s - 1], long_recv_sem.at[h * 4 + s - 1])
            value = value + long_in[h * 4 + s - 1].astype(jnp.float32)
        at = h * 4 + s
        long_out[at] = value.astype(SUM_TYPE)
        send(long_out.at[at], long_in.at[at], long_send_sem.at[at], long_recv_sem.at[at], at_z(way))

    def short_step(h, s):
        way = 2 * (h % 2) - 1
        value = partial[(way * (3 - s)) % NZ, :, features(h)]
        if s:
            arrived(short_in.at[h * 3 + s - 1], short_recv_sem.at[h * 3 + s - 1])
            value = value + short_in[h * 3 + s - 1].astype(jnp.float32)
        at = h * 3 + s
        short_out[at] = value.astype(SUM_TYPE)
        send(short_out.at[at], short_in.at[at], short_send_sem.at[at], short_recv_sem.at[at], at_z(way))

    make_transport(4)
    make_transport(3)
    for n in range(CHUNKS // 2):
        weigh(4, 3, n)
        for h in (2 * n, 2 * n + 1):
            long_step(h, 0)
        short_step(2 * n + 1, 0)
    make_transport(-3)
    make_transport(2)
    for n in range(CHUNKS // 2):
        weigh(-3, 2, n)
        short_step(2 * n, 0)
    for h in range(CHUNKS):
        long_step(h, 1)
        if h % 2:
            short_step(h, 1)
    make_transport(-2)
    make_transport(1)
    for n in range(CHUNKS // 2):
        weigh(-2, 1, n)
    for n in range(CHUNKS // 2):
        short_step(2 * n, 1)
        for h in (2 * n, 2 * n + 1):
            long_step(h, 2)
        short_step(2 * n + 1, 2)
    make_transport(-1)
    make_transport(0)
    start_total(3)
    for n in range(CHUNKS // 2):
        weigh(-1, 0, n)
        short_step(2 * n, 2)
    for h in range(CHUNKS):
        long_step(h, 3)
    col_vec[...] = to_columns(finish_total(3))
    mass = col_vec[pl.ds(pl.multiple_of(z * OWN, OWN), OWN), :][:, :1]
    for h in range(CHUNKS):
        arrived(short_in.at[h * 3 + 2], short_recv_sem.at[h * 3 + 2])
        weighted = partial[0, :, features(h)] + short_in[h * 3 + 2].astype(jnp.float32)
        arrived(long_in.at[h * 4 + 3], long_recv_sem.at[h * 4 + 3])
        weighted = weighted + long_in[h * 4 + 3].astype(jnp.float32)
        grad[:, features(h)] = (mass * cent[:, features(h)] - weighted) * (KB / ROWS)

    for copy in pending:
        copy.wait_send()


def per_device(stream, sample_index, centroids, first_moment, second_moment):
    f32 = jnp.float32
    scratch = [
        pltpu.VMEM((STREAM, E), jnp.bfloat16),
        pltpu.VMEM((NR, E), jnp.bfloat16),
        pltpu.VMEM((COLS, E), jnp.bfloat16),
        pltpu.VMEM((COLS, NR), f32),
        pltpu.VMEM((COLS, NR), jnp.bfloat16),
        pltpu.VMEM((COLS, BLK), f32),
        pltpu.VMEM((COLS, BLK), f32),
        pltpu.VMEM((COLS, BLK), f32),
        pltpu.VMEM((COLS, BLK), f32),
        pltpu.VMEM((4, SLOTS, BLK), f32),
        pltpu.VMEM((4, SLOTS, BLK), f32),
        pltpu.VMEM((4, SLOTS, BLK), f32),
        pltpu.VMEM((4, PLANE, SLOTS, BLK), f32),
        pltpu.VMEM((SLOTS, BLK), f32),
        pltpu.VMEM((2, COLS), f32),
        pltpu.VMEM((3, 1, COLS), f32),
        pltpu.VMEM((NZ, 2, COLS), f32),
        pltpu.VMEM((3, NZ, 1, COLS), f32),
        pltpu.VMEM((NZ, OWN, E), f32),
        pltpu.VMEM((4 * CHUNKS, OWN, CHUNK), SUM_TYPE),
        pltpu.VMEM((3 * CHUNKS, OWN, CHUNK), SUM_TYPE),
        pltpu.VMEM((4 * CHUNKS, OWN, CHUNK), SUM_TYPE),
        pltpu.VMEM((3 * CHUNKS, OWN, CHUNK), SUM_TYPE),
        pltpu.SemaphoreType.DMA((64,)),
        pltpu.SemaphoreType.DMA((SLOTS, PARTS)),
        pltpu.SemaphoreType.DMA,
        pltpu.SemaphoreType.DMA,
        pltpu.SemaphoreType.DMA((14,)),
        pltpu.SemaphoreType.DMA((NZ, 2)),
        pltpu.SemaphoreType.DMA((4,)),
        pltpu.SemaphoreType.DMA((4,)),
        pltpu.SemaphoreType.DMA((4, PLANE - 1)),
        pltpu.SemaphoreType.DMA((4, PLANE)),
        pltpu.SemaphoreType.DMA((4, NZ - 1)),
        pltpu.SemaphoreType.DMA((4, NZ)),
        pltpu.SemaphoreType.DMA((4 * CHUNKS,)),
        pltpu.SemaphoreType.DMA((4 * CHUNKS,)),
        pltpu.SemaphoreType.DMA((3 * CHUNKS,)),
        pltpu.SemaphoreType.DMA((3 * CHUNKS,)),
        pltpu.SemaphoreType.DMA,
    ]
    gradient = pl.pallas_call(
        kernel,
        out_shape=jax.ShapeDtypeStruct((OWN, E), f32),
        in_specs=[pl.BlockSpec(memory_space=pl.ANY)] + [pl.BlockSpec(memory_space=pltpu.VMEM)] * 2,
        out_specs=pl.BlockSpec(memory_space=pltpu.VMEM),
        scratch_shapes=scratch,
        compiler_params=pltpu.CompilerParams(
            collective_id=0, has_side_effects=True, vmem_limit_bytes=56 * 1024 * 1024
        ),
        cost_estimate=pl.CostEstimate(
            flops=4 * NR * COLS * E, bytes_accessed=4 * 1024 * 1024, transcendentals=3 * NR * COLS
        ),
        name="balanced_kmeans",
    )(stream, sample_index.reshape(ND // BLK, BLK), centroids)
    new_first = beta_one * first_moment + (1.0 - beta_one) * gradient
    new_second = beta_two * second_moment + (1.0 - beta_two) * gradient * gradient
    new_centroids = centroids - step_rate * new_first / (jnp.sqrt(new_second) + epsilon)
    return (new_centroids, new_first, new_second)


def solution(mesh):
    cut = P(("cent", "dp"), None)
    return jax.shard_map(
        per_device,
        mesh=mesh,
        in_specs=(P("dp", None), P("dp"), cut, cut, cut),
        out_specs=(cut, cut, cut),
        check_vma=False,
    )
```
